32 devices in a mesh: grp: 2 (over y), seq: 8 (over z, x), pd: 2 (over core).
Axes of the slice: x: 2, y: 2, z: 4, core: 2. Of those that a mesh axis runs over, the one named last changes fastest.
Arguments:
- new_kv: bfloat16 [4, 1024, 2048], P('grp', ('seq', 'pd')), parts along dimension 0, may hold values from -6 to 6
- old_keys: bfloat16 [8, 2048, 256], P('seq', 'grp'), parts along dimension 1, may hold values from -18 to 18
- old_values: bfloat16 [8, 2048, 256], P('seq', 'grp'), parts along dimension 1, may hold values from -6 to 6
- suffix_keys: bfloat16 [2, 8, 128, 32, 256], P('pd', 'seq', 'grp'), parts along dimension 2, may hold values from -28 to 28
- suffix_values: bfloat16 [2, 8, 128, 32, 256], P('pd', 'seq', 'grp'), parts along dimension 2, may hold values from -6 to 6
- queries: bfloat16 [128, 8192], P(('seq', 'pd'), 'grp'), parts along dimension 1, may hold values from -18 to 18
- lengths: int32 [256], P('grp'), parts along dimension 0, may hold values from 1 to 32, as said below
- assign: int32 [256], P('grp'), parts along dimension 0, may hold values from 0 to 1
Outputs:
- new_cache: bfloat16 [2, 8, 16, 128, 256], P(None, 'seq', 'grp', 'pd'), parts along dimension 2
- attention: bfloat16 [128, 8192], P(('seq', 'pd'), 'grp'), parts along dimension 1
The draws below stay inside these ranges and needn't reach their ends.
There are 2 independent parts, one for each index of `grp`. The reference program is written for one: setup_inputs(seed, part) draws one part's arguments, and reference() takes and returns one part's arrays. A program takes and returns all parts, laid end to end along the dimension named above; each array names one. Nothing has to cross between parts.
Inputs may be any that keep to these rules, and one draw needn't show every extreme that they name: `lengths`: suffix tokens of each request, its new token included; some request has exactly 32. `assign`: which of the 2 prefixes each request continues.
All inputs are finite; a program needn't handle non-finite values.
Results may differ from the reference program's by a relative error of at most 0.0048.
Values may be sent and summed in bfloat16 or wider, within the bound.
No kernel may reach another device: no remote copies, remote signals or barrier semaphores. Data moves between devices by JAX's collectives and lax.ppermute only.
A program may use at most 64 MiB of HBM per device.

```python
import jax
import jax.numpy as jnp
from jax import lax

HD = 128
KVH = 16
NQH = 32
NPFX = 2
REQ_DEV = 8
LSUF = 32
QPK = 2
SUB = 1
HPD = 2
GRPS = 8
PREFIX = 1024
PLEN = 512
REQUESTS = 128
SUF_REQ = 64
N_SEQ = 8
N_PD = 2


def draw_lengths(key, part):
    key = jax.random.fold_in(key, 11)
    first_key, second_key = jax.random.split(key)
    drawn = jax.random.randint(first_key, (REQUESTS,), 1, LSUF + 1)
    picked = jax.random.permutation(second_key, REQUESTS)[:max(REQUESTS // 16, 1)]
    return drawn.at[picked].set(LSUF).astype(jnp.int32)


def place_ends(values, own_key, least, high):
    shape = values.shape
    spot = [jax.random.randint(jax.random.fold_in(own_key, axis), (), 0, shape[axis]) for axis in range(len(shape))]
    values = values.at[tuple(spot)].set(least)
    longest = shape.index(max(shape))
    spot[longest] = (spot[longest] + 1) % shape[longest]
    return values.at[tuple(spot)].set(high)


def shard_levels(key, dims, cuts, least, high):
    factor_of, own = 1.0, jax.random.fold_in(key, 6)
    for position, shards_of in cuts:
        heights = jnp.exp(jax.random.uniform(jax.random.fold_in(own, position), (shards_of,), jnp.float32, least / len(cuts), high / len(cuts)))
        factor_of = factor_of * jnp.repeat(heights, dims[position] // shards_of).reshape([-1 if axis == position else 1 for axis in range(len(dims))])
    return factor_of


def bell_draw(own_key, shape, width, reach, cuts=(), kind=jnp.bfloat16):
    entries = width * jax.random.normal(own_key, shape, jnp.float32)
    if cuts:
        entries = entries * shard_levels(own_key, shape, cuts, -0.22, 0.18)
    return jnp.clip(entries, -reach, reach).astype(kind)


def setup_inputs(seed: int = 0, part: int = 0) -> dict:
    seeds = jax.random.split(jax.random.key(seed), 9)
    own_keys = jax.random.split(jax.random.fold_in(seeds[8], part), 9)
    return {
        "new_kv": bell_draw(own_keys[0], (2, PREFIX, KVH * HD), 1.0, 6.0, ((1, 16),)),
        "old_keys": bell_draw(own_keys[1], (N_SEQ, PREFIX // SUB, HPD * HD), 3.0, 18.0, ((0, 8),)),
        "old_values": bell_draw(own_keys[2], (N_SEQ, PREFIX // SUB, HPD * HD), 1.0, 6.0, ((0, 8),)),
        "suffix_keys": bell_draw(own_keys[3], (N_PD, N_SEQ, SUF_REQ, LSUF, HPD * HD), 4.8, 28.0, ((0, 2), (1, 8))),
        "suffix_values": bell_draw(own_keys[4], (N_PD, N_SEQ, SUF_REQ, LSUF, HPD * HD), 1.0, 6.0, ((0, 2), (1, 8))),
        "queries": bell_draw(own_keys[5], (REQUESTS, NQH * HD), 3.0, 18.0, ((0, 16),)),
        "lengths": draw_lengths(jax.random.fold_in(jax.random.fold_in(seeds[8], part), 71), part),
        "assign": place_ends(jax.random.randint(own_keys[7], (REQUESTS,), 0, NPFX), jax.random.fold_in(own_keys[7], 1), 0, NPFX - 1).astype(jnp.int32),
    }


softcap = 50.0
query_scale = 1.0 / 12.0


def rotary(key_rows, positions):
    head_width = key_rows.shape[-1]
    halfway = head_width // 2
    inverse = 10000.0 ** (-2.0 * jnp.arange(halfway).astype(jnp.float32) / head_width)
    angles = positions.astype(jnp.float32)[:, None] * inverse[None, :]
    angles = jnp.concatenate([angles, angles], axis=1)
    values = key_rows.astype(jnp.float32)
    turned = jnp.concatenate([-values[..., halfway:], values[..., :halfway]], axis=-1)
    return values * jnp.cos(angles)[:, None, :] + turned * jnp.sin(angles)[:, None, :]


def capped(scores):
    return softcap * jnp.tanh(scores * query_scale / softcap)


def unpack_cache(stored):
    shaped = stored.reshape(SUB, GRPS, PREFIX // SUB, HPD * HD)
    return shaped.transpose(2, 0, 1, 3).reshape(PREFIX, KVH * HD)


def unpack_suffix(stored):
    shaped = stored.reshape(N_PD, SUB, GRPS, GRPS, REQ_DEV, LSUF, HPD * HD)
    return shaped.transpose(1, 3, 0, 4, 5, 2, 6).reshape(REQUESTS, LSUF, KVH * HD)


def reference(new_kv, old_keys, old_values, suffix_keys, suffix_values, queries, lengths, assign):
    positions = jnp.arange(PREFIX, dtype=jnp.int32) % PLEN
    new_keys = rotary(new_kv[0].reshape(PREFIX, KVH, HD), positions).astype(jnp.bfloat16)
    new_keys = new_keys.reshape(PREFIX, KVH * HD)
    stacked = jnp.stack([new_keys, new_kv[1]])
    blocks_out = PREFIX // (N_SEQ * SUB)
    stacked = stacked.reshape(2, N_SEQ, blocks_out, SUB, GRPS, HPD * HD)
    new_cache = stacked.transpose(0, 3, 4, 1, 2, 5).reshape(2, N_SEQ, N_SEQ, blocks_out, HPD * HD)

    prefix_keys = unpack_cache(old_keys)
    prefix_values = unpack_cache(old_values)
    recent_keys = unpack_suffix(suffix_keys)
    recent_values = unpack_suffix(suffix_values)
    token_prefix = jnp.arange(PREFIX, dtype=jnp.int32) // PLEN
    visible = assign[:, None] == token_prefix[None, :]
    live_slots = jnp.arange(LSUF, dtype=jnp.int32)[None, :] < lengths[:, None]
    query_heads = queries.reshape(REQUESTS, KVH, QPK, HD)

    def per_head(head_index):
        head_query = lax.dynamic_index_in_dim(query_heads, head_index, 1, keepdims=False).astype(jnp.float32)
        head_keys = lax.dynamic_slice_in_dim(prefix_keys, head_index * HD, HD, 1).astype(jnp.float32)
        head_values = lax.dynamic_slice_in_dim(prefix_values, head_index * HD, HD, 1).astype(jnp.float32)
        scores = capped(jnp.einsum('rqd,xd->rqx', head_query, head_keys))
        weights = jnp.where(visible[:, None, :], jnp.exp(scores), 0.0)
        totals = jnp.sum(weights, axis=-1)
        rounded = lax.optimization_barrier(weights.astype(jnp.bfloat16)).astype(jnp.float32)
        numerators = jnp.einsum('rqx,xd->rqd', rounded, head_values)
        suffix_k = lax.dynamic_slice_in_dim(recent_keys, head_index * HD, HD, 2).astype(jnp.float32)
        suffix_v = lax.dynamic_slice_in_dim(recent_values, head_index * HD, HD, 2).astype(jnp.float32)
        recent_scores = capped(jnp.einsum('rqd,rpd->rqp', head_query, suffix_k))
        recent_weights = jnp.where(live_slots[:, None, :], jnp.exp(recent_scores), 0.0)
        totals = totals + jnp.sum(recent_weights, axis=-1)
        recent_rounded = lax.optimization_barrier(recent_weights.astype(jnp.bfloat16)).astype(jnp.float32)
        numerators = numerators + jnp.einsum('rqp,rpd->rqd', recent_rounded, suffix_v)
        return (numerators / totals[..., None]).astype(jnp.bfloat16)

    attended = lax.map(per_head, jnp.arange(KVH, dtype=jnp.int32))
    attention = attended.transpose(1, 0, 2, 3).reshape(REQUESTS, NQH * HD)
    return new_cache, attention
```

```python
import functools
import math

import jax
import jax.numpy as jnp
import numpy as np
from jax import lax
from jax.experimental import pallas as pl
from jax.experimental.pallas import tpu as pltpu
from jax.sharding import PartitionSpec as P

HD = 128
KVH = 16
NQH = 32
NPFX = 2


softcap = 50.0
query_scale = 1.0 / 12.0


def rotary(key_rows, positions):
    head_width = key_rows.shape[-1]
    halfway = head_width // 2
    inverse = 10000.0 ** (-2.0 * jnp.arange(halfway).astype(jnp.float32) / head_width)
    angles = positions.astype(jnp.float32)[:, None] * inverse[None, :]
    angles = jnp.concatenate([angles, angles], axis=1)
    values = key_rows.astype(jnp.float32)
    turned = jnp.concatenate([-values[..., halfway:], values[..., :halfway]], axis=-1)
    return values * jnp.cos(angles)[:, None, :] + turned * jnp.sin(angles)[:, None, :]


def capped(scores):
    return softcap * jnp.tanh(scores * query_scale / softcap)


def general(new_kv, old_keys, old_values, suffix_keys, suffix_values, queries, lengths, assign):
    seq_count = lax.axis_size("seq")
    core_count = lax.axis_size("pd")
    seq_place = lax.axis_index("seq")
    core_place = lax.axis_index("pd")
    per_kv = NQH // KVH
    sub_blocks = max(seq_count // KVH, 1)
    heads_here = max(KVH // seq_count, 1)
    head_groups = KVH // heads_here
    prefix_rows = new_kv.shape[1]
    request_rows = queries.shape[0]
    prefix_length = prefix_rows * seq_count * core_count // NPFX
    group_width = heads_here * per_kv * HD
    positions = (
        (seq_place * core_count + core_place) * prefix_rows
        + jnp.arange(prefix_rows, dtype=jnp.int32)
    ) % prefix_length
    rotated = rotary(new_kv[0].reshape(prefix_rows, KVH, HD), positions).astype(jnp.bfloat16)
    rotated = rotated.reshape(prefix_rows, KVH * HD)
    outgoing = jnp.stack([rotated, new_kv[1]]).reshape(
        2, prefix_rows // sub_blocks, seq_count, heads_here * HD
    )
    arrived = lax.all_to_all(outgoing, "seq", split_axis=2, concat_axis=1, tiled=True)
    new_cache = arrived.reshape(2, 1, seq_count, prefix_rows // sub_blocks, heads_here * HD)
    head_group = seq_place % head_groups
    token_block = seq_place // head_groups
    half_rows = seq_count * request_rows
    gathered = lax.all_gather(queries, "seq", axis=0, tiled=True)
    own_queries = lax.dynamic_slice_in_dim(gathered, head_group * group_width, group_width, 1)
    query_blocks = own_queries.reshape(half_rows, heads_here, per_kv, HD)
    own_assign = lax.dynamic_index_in_dim(
        assign.reshape(seq_count, core_count, request_rows), core_place, 1, keepdims=False
    ).reshape(half_rows)
    own_lengths = lax.dynamic_index_in_dim(
        lengths.reshape(seq_count, core_count, request_rows), core_place, 1, keepdims=False
    ).reshape(half_rows)
    prefix_keys = old_keys[0].reshape(-1, heads_here, HD)
    prefix_values = old_values[0].reshape(-1, heads_here, HD)
    token_count = prefix_keys.shape[0]
    token_prefix = (
        jnp.arange(token_count, dtype=jnp.int32) * sub_blocks + token_block
    ) // prefix_length
    block_rows = math.gcd(half_rows, 256)

    def prefix_block(block_index):
        row_start = block_index * block_rows
        query_part = lax.dynamic_slice_in_dim(query_blocks, row_start, block_rows, 0)
        assign_part = lax.dynamic_slice_in_dim(own_assign, row_start, block_rows, 0)
        scores = capped(
            jnp.einsum(
                "rhqd,thd->rhqt", query_part, prefix_keys, preferred_element_type=jnp.float32
            )
        )
        allowed = (assign_part[:, None] == token_prefix[None, :])[:, None, None, :]
        weights = jnp.where(allowed, jnp.exp(scores), 0.0)
        totals = jnp.sum(weights, axis=-1)
        numerators = jnp.einsum(
            "rhqt,thd->rhqd",
            weights.astype(jnp.bfloat16),
            prefix_values,
            preferred_element_type=jnp.float32,
        )
        return (totals, numerators)

    totals, numerators = lax.map(prefix_block, jnp.arange(half_rows // block_rows, dtype=jnp.int32))
    totals = totals.reshape(half_rows, heads_here, per_kv)
    numerators = numerators.reshape(half_rows, heads_here, per_kv, HD)
    suffix_rows = head_groups * request_rows
    suffix_start = token_block * suffix_rows
    suffix_query = lax.dynamic_slice_in_dim(query_blocks, suffix_start, suffix_rows, 0)
    suffix_length = lax.dynamic_slice_in_dim(own_lengths, suffix_start, suffix_rows, 0)
    recent_keys = suffix_keys[0, 0].reshape(suffix_rows, -1, heads_here, HD)
    recent_values = suffix_values[0, 0].reshape(suffix_rows, -1, heads_here, HD)
    recent_scores = capped(
        jnp.einsum("rhqd,rphd->rhqp", suffix_query, recent_keys, preferred_element_type=jnp.float32)
    )
    live_slots = jnp.arange(recent_keys.shape[1], dtype=jnp.int32)[None, :] < suffix_length[:, None]
    recent_weights = jnp.where(live_slots[:, None, None, :], jnp.exp(recent_scores), 0.0)
    recent_totals = jnp.sum(recent_weights, axis=-1)
    recent_numerators = jnp.einsum(
        "rhqp,rphd->rhqd",
        recent_weights.astype(jnp.bfloat16),
        recent_values,
        preferred_element_type=jnp.float32,
    )
    totals = lax.dynamic_update_slice_in_dim(
        totals,
        lax.dynamic_slice_in_dim(totals, suffix_start, suffix_rows, 0) + recent_totals,
        suffix_start,
        0,
    )
    numerators = lax.dynamic_update_slice_in_dim(
        numerators,
        lax.dynamic_slice_in_dim(numerators, suffix_start, suffix_rows, 0) + recent_numerators,
        suffix_start,
        0,
    )
    back_numerators, back_totals = (
        lax.all_to_all(
            numerators.reshape(seq_count, request_rows, group_width),
            "seq",
            split_axis=0,
            concat_axis=0,
            tiled=True,
        ),
        lax.all_to_all(
            totals.reshape(seq_count, request_rows, heads_here * per_kv),
            "seq",
            split_axis=0,
            concat_axis=0,
            tiled=True,
        ),
    )
    back_numerators = back_numerators.reshape(
        sub_blocks, head_groups, request_rows, heads_here * per_kv, HD
    ).sum(0)
    back_totals = back_totals.reshape(
        sub_blocks, head_groups, request_rows, heads_here * per_kv
    ).sum(0)
    attention = (
        (back_numerators / back_totals[..., None])
        .transpose(1, 0, 2, 3)
        .reshape(request_rows, NQH * HD)
    )
    return (new_cache, attention.astype(jnp.bfloat16))


def rotate_kernel(seq_count, core_count, prefix_length, rates_ref, kv_ref, *out_refs):
    place = lax.axis_index("seq")
    rows = kv_ref.shape[1]
    width = kv_ref.shape[2] // seq_count
    first = (place * core_count + lax.axis_index("pd")) * rows
    position = (first + lax.broadcasted_iota(jnp.int32, (rows, HD), 0)) % prefix_length
    angles = position.astype(jnp.float32) * rates_ref[...]
    cosine = jnp.cos(angles)
    sine = jnp.sin(angles)
    sine = jnp.where(lax.broadcasted_iota(jnp.int32, (rows, HD), 1) < HD // 2, -sine, sine)
    for k in range(seq_count):
        block = jnp.bitwise_xor(place, k) * width
        for h in range(width // HD):
            columns = pl.ds(pl.multiple_of(block + h * HD, HD), HD)
            keys = kv_ref[0, :, columns].astype(jnp.float32)
            turned = pltpu.roll(keys, HD // 2, 1)
            out_refs[k][0, :, h * HD : (h + 1) * HD] = (keys * cosine + turned * sine).astype(jnp.bfloat16)
            out_refs[k][1, :, h * HD : (h + 1) * HD] = kv_ref[1, :, columns]


def rotate_blocks(new_kv, seq_count, core_count):
    _, rows, columns = new_kv.shape
    width = columns // seq_count
    prefix_length = rows * seq_count * core_count // NPFX
    rates = 10000.0 ** (-2.0 * (np.arange(HD) % (HD // 2)) / HD)
    return pl.pallas_call(
        functools.partial(rotate_kernel, seq_count, core_count, prefix_length),
        out_shape=[jax.ShapeDtypeStruct((2, rows, width), jnp.bfloat16)] * seq_count,
        in_specs=[pl.BlockSpec(memory_space=pltpu.VMEM)] * 2,
        out_specs=[pl.BlockSpec(memory_space=pltpu.VMEM)] * seq_count,
        cost_estimate=pl.CostEstimate(
            flops=6 * rows * columns, bytes_accessed=8 * rows * columns, transcendentals=2 * rows * HD
        ),
    )(jnp.asarray(rates.astype(np.float32)).reshape(1, HD), new_kv)


def assemble_kernel(seq_count, *refs):
    *pieces, out_ref, sems = refs
    place = lax.axis_index("seq")
    copies = []
    for k in range(seq_count):
        for v in range(2):
            copies.append(
                pltpu.make_async_copy(
                    pieces[k].at[v], out_ref.at[v, 0, jnp.bitwise_xor(place, k)], sems.at[k, v]
                )
            )
            copies[-1].start()
    for copy in copies:
        copy.wait()


def assemble(pieces):
    count = len(pieces)
    _, rows, width = pieces[0].shape
    return pl.pallas_call(
        functools.partial(assemble_kernel, count),
        out_shape=jax.ShapeDtypeStruct((2, 1, count, rows, width), jnp.bfloat16),
        in_specs=[pl.BlockSpec(memory_space=pl.ANY)] * count,
        out_specs=pl.BlockSpec(memory_space=pl.ANY),
        scratch_shapes=[pltpu.SemaphoreType.DMA((count, 2))],
        cost_estimate=pl.CostEstimate(
            flops=0, bytes_accessed=8 * count * rows * width, transcendentals=0
        ),
    )(*pieces)


def weigh(scores):
    return jnp.exp2((softcap * math.log2(math.e)) * jnp.tanh(scores * (query_scale / softcap)))


NT = (((1,), (1,)), ((), ()))
NN = (((1,), (0,)), ((), ()))


def attend_kernel(q_ref, keys_ref, values_ref, skeys_ref, svalues_ref, assign_ref, lengths_ref, out_ref, num_ref, total_ref):
    requests = q_ref.shape[0]
    per_kv = NQH // KVH
    heads_here = keys_ref.shape[2] // HD
    length = keys_ref.shape[1] // NPFX
    slots = skeys_ref.shape[3]
    span = 8
    which = assign_ref[...]
    for h in range(heads_here):
        columns = slice(h * HD, (h + 1) * HD)
        query = jnp.concatenate(
            [q_ref[:, (h * per_kv + j) * HD : (h * per_kv + j + 1) * HD] for j in range(per_kv)], axis=0
        )
        scores = lax.dot_general(query, keys_ref[0, :length, columns], NT, preferred_element_type=jnp.float32)
        for p in range(1, NPFX):
            other = lax.dot_general(
                query, keys_ref[0, p * length : (p + 1) * length, columns], NT, preferred_element_type=jnp.float32
            )
            scores = jnp.where(which == p, other, scores)
        weights = weigh(scores)
        total = jnp.sum(weights, axis=1, keepdims=True)
        numerator = None
        for p in range(NPFX):
            part = lax.dot_general(
                jnp.where(which == p, weights, 0.0).astype(jnp.bfloat16),
                values_ref[0, p * length : (p + 1) * length, columns],
                NN,
                preferred_element_type=jnp.float32,
            )
            numerator = part if numerator is None else numerator + part
        query32 = query.astype(jnp.float32)
        column = lax.broadcasted_iota(jnp.int32, (span * per_kv, span * slots), 1)
        low = lax.broadcasted_iota(jnp.int32, (span * per_kv, span * slots), 0) % span * slots
        num_ref[...] = numerator
        total_ref[...] = jnp.broadcast_to(total, total_ref.shape)
        for b in range(requests // span):
            picked = [slice(j * requests + b * span, j * requests + (b + 1) * span) for j in range(per_kv)]
            part = jnp.concatenate([query32[rows] for rows in picked], axis=0).astype(jnp.bfloat16)
            skeys = skeys_ref[0, 0, b * span : (b + 1) * span, :, columns].reshape(span * slots, HD)
            svalues = svalues_ref[0, 0, b * span : (b + 1) * span, :, columns].reshape(span * slots, HD)
            recent = weigh(lax.dot_general(part, skeys, NT, preferred_element_type=jnp.float32))
            live = jnp.concatenate([lengths_ref[rows] for rows in picked], axis=0)
            recent = jnp.where((column >= low) & (column < low + live), recent, 0.0)
            more = jnp.sum(recent, axis=1, keepdims=True)
            added = lax.dot_general(recent.astype(jnp.bfloat16), svalues, NN, preferred_element_type=jnp.float32)
            for j, rows in enumerate(picked):
                num_ref[rows] += added[j * span : (j + 1) * span]
                total_ref[rows] += jnp.broadcast_to(more[j * span : (j + 1) * span], (span, HD))
        result = (num_ref[...] / total_ref[...]).astype(jnp.bfloat16)
        for j in range(per_kv):
            out_ref[:, (h * per_kv + j) * HD : (h * per_kv + j + 1) * HD] = result[j * requests : (j + 1) * requests]


def attend(queries, old_keys, old_values, suffix_keys, suffix_values, assign, lengths):
    requests, width = queries.shape
    per_kv = NQH // KVH
    tall = per_kv * requests
    tokens = old_keys.shape[1]
    return pl.pallas_call(
        attend_kernel,
        out_shape=jax.ShapeDtypeStruct((requests, width), jnp.bfloat16),
        in_specs=[pl.BlockSpec(memory_space=pltpu.VMEM)] * 7,
        out_specs=pl.BlockSpec(memory_space=pltpu.VMEM),
        scratch_shapes=[pltpu.VMEM((tall, HD), jnp.float32), pltpu.VMEM((tall, HD), jnp.float32)],
        compiler_params=pltpu.CompilerParams(vmem_limit_bytes=24 * 2**20),
        cost_estimate=pl.CostEstimate(
            flops=4 * requests * width * tokens * 2, bytes_accessed=3 * 2**20, transcendentals=requests * width * 8
        ),
    )(queries, old_keys, old_values, suffix_keys, suffix_values, assign, lengths)


def local(new_kv, old_keys, old_values, suffix_keys, suffix_values, queries, lengths, assign):
    seq_count = lax.axis_size("seq")
    core_count = lax.axis_size("pd")
    if seq_count > KVH or seq_count & (seq_count - 1):
        return general(new_kv, old_keys, old_values, suffix_keys, suffix_values, queries, lengths, assign)
    core_place = lax.axis_index("pd")
    per_kv = NQH // KVH
    request_rows = queries.shape[0]
    half_rows = seq_count * request_rows
    group_width = queries.shape[1] // seq_count
    asked = lax.all_to_all(
        queries.reshape(request_rows, seq_count, group_width).transpose(1, 0, 2), "seq", 0, 0, tiled=True
    )
    blocks = rotate_blocks(new_kv, seq_count, core_count)
    pieces = [blocks[0]]
    for k in range(1, seq_count):
        pieces.append(lax.ppermute(blocks[k], "seq", [(i, i ^ k) for i in range(seq_count)]))

    def own(values):
        mine = lax.dynamic_index_in_dim(
            values.reshape(seq_count, core_count, request_rows), core_place, 1, keepdims=False
        ).reshape(half_rows)
        return jnp.tile(mine, per_kv)[:, None]

    attended = attend(
        asked.reshape(half_rows, group_width),
        old_keys,
        old_values,
        suffix_keys,
        suffix_values,
        own(assign),
        own(lengths),
    )
    back = lax.all_to_all(attended.reshape(seq_count, request_rows, group_width), "seq", 0, 0, tiled=True)
    attention = back.transpose(1, 0, 2).reshape(request_rows, NQH * HD)
    return (assemble(pieces), attention)


def solution(mesh):
    return jax.shard_map(
        local,
        mesh=mesh,
        in_specs=(
            P("grp", ("seq", "pd"), None),
            P("seq", "grp", None),
            P("seq", "grp", None),
            P("pd", "seq", "grp", None, None),
            P("pd", "seq", "grp", None, None),
            P(("seq", "pd"), "grp"),
            P("grp"),
            P("grp"),
        ),
        out_specs=(P(None, "seq", "grp", "pd", None), P(("seq", "pd"), "grp")),
        check_vma=False,
    )
```

```python
import functools
import math

import jax
import jax.numpy as jnp
import numpy as np
from jax import lax
from jax.experimental import pallas as pl
from jax.experimental.pallas import tpu as pltpu
from jax.sharding import PartitionSpec as P

HD = 128
KVH = 16
NQH = 32
NPFX = 2


softcap = 50.0
query_scale = 1.0 / 12.0


def rotary(key_rows, positions):
    head_width = key_rows.shape[-1]
    halfway = head_width // 2
    inverse = 10000.0 ** (-2.0 * jnp.arange(halfway).astype(jnp.float32) / head_width)
    angles = positions.astype(jnp.float32)[:, None] * inverse[None, :]
    angles = jnp.concatenate([angles, angles], axis=1)
    values = key_rows.astype(jnp.float32)
    turned = jnp.concatenate([-values[..., halfway:], values[..., :halfway]], axis=-1)
    return values * jnp.cos(angles)[:, None, :] + turned * jnp.sin(angles)[:, None, :]


def capped(scores):
    return softcap * jnp.tanh(scores * query_scale / softcap)


def general(new_kv, old_keys, old_values, suffix_keys, suffix_values, queries, lengths, assign):
    seq_count = lax.axis_size("seq")
    core_count = lax.axis_size("pd")
    seq_place = lax.axis_index("seq")
    core_place = lax.axis_index("pd")
    per_kv = NQH // KVH
    sub_blocks = max(seq_count // KVH, 1)
    heads_here = max(KVH // seq_count, 1)
    head_groups = KVH // heads_here
    prefix_rows = new_kv.shape[1]
    request_rows = queries.shape[0]
    prefix_length = prefix_rows * seq_count * core_count // NPFX
    group_width = heads_here * per_kv * HD
    positions = (
        (seq_place * core_count + core_place) * prefix_rows
        + jnp.arange(prefix_rows, dtype=jnp.int32)
    ) % prefix_length
    rotated = rotary(new_kv[0].reshape(prefix_rows, KVH, HD), positions).astype(jnp.bfloat16)
    rotated = rotated.reshape(prefix_rows, KVH * HD)
    outgoing = jnp.stack([rotated, new_kv[1]]).reshape(
        2, prefix_rows // sub_blocks, seq_count, heads_here * HD
    )
    arrived = lax.all_to_all(outgoing, "seq", split_axis=2, concat_axis=1, tiled=True)
    new_cache = arrived.reshape(2, 1, seq_count, prefix_rows // sub_blocks, heads_here * HD)
    head_group = seq_place % head_groups
    token_block = seq_place // head_groups
    half_rows = seq_count * request_rows
    gathered = lax.all_gather(queries, "seq", axis=0, tiled=True)
    own_queries = lax.dynamic_slice_in_dim(gathered, head_group * group_width, group_width, 1)
    query_blocks = own_queries.reshape(half_rows, heads_here, per_kv, HD)
    own_assign = lax.dynamic_index_in_dim(
        assign.reshape(seq_count, core_count, request_rows), core_place, 1, keepdims=False
    ).reshape(half_rows)
    own_lengths = lax.dynamic_index_in_dim(
        lengths.reshape(seq_count, core_count, request_rows), core_place, 1, keepdims=False
    ).reshape(half_rows)
    prefix_keys = old_keys[0].reshape(-1, heads_here, HD)
    prefix_values = old_values[0].reshape(-1, heads_here, HD)
    token_count = prefix_keys.shape[0]
    token_prefix = (
        jnp.arange(token_count, dtype=jnp.int32) * sub_blocks + token_block
    ) // prefix_length
    block_rows = math.gcd(half_rows, 256)

    def prefix_block(block_index):
        row_start = block_index * block_rows
        query_part = lax.dynamic_slice_in_dim(query_blocks, row_start, block_rows, 0)
        assign_part = lax.dynamic_slice_in_dim(own_assign, row_start, block_rows, 0)
        scores = capped(
            jnp.einsum(
                "rhqd,thd->rhqt", query_part, prefix_keys, preferred_element_type=jnp.float32
            )
        )
        allowed = (assign_part[:, None] == token_prefix[None, :])[:, None, None, :]
        weights = jnp.where(allowed, jnp.exp(scores), 0.0)
        totals = jnp.sum(weights, axis=-1)
        numerators = jnp.einsum(
            "rhqt,thd->rhqd",
            weights.astype(jnp.bfloat16),
            prefix_values,
            preferred_element_type=jnp.float32,
        )
        return (totals, numerators)

    totals, numerators = lax.map(prefix_block, jnp.arange(half_rows // block_rows, dtype=jnp.int32))
    totals = totals.reshape(half_rows, heads_here, per_kv)
    numerators = numerators.reshape(half_rows, heads_here, per_kv, HD)
    suffix_rows = head_groups * request_rows
    suffix_start = token_block * suffix_rows
    suffix_query = lax.dynamic_slice_in_dim(query_blocks, suffix_start, suffix_rows, 0)
    suffix_length = lax.dynamic_slice_in_dim(own_lengths, suffix_start, suffix_rows, 0)
    recent_keys = suffix_keys[0, 0].reshape(suffix_rows, -1, heads_here, HD)
    recent_values = suffix_values[0, 0].reshape(suffix_rows, -1, heads_here, HD)
    recent_scores = capped(
        jnp.einsum("rhqd,rphd->rhqp", suffix_query, recent_keys, preferred_element_type=jnp.float32)
    )
    live_slots = jnp.arange(recent_keys.shape[1], dtype=jnp.int32)[None, :] < suffix_length[:, None]
    recent_weights = jnp.where(live_slots[:, None, None, :], jnp.exp(recent_scores), 0.0)
    recent_totals = jnp.sum(recent_weights, axis=-1)
    recent_numerators = jnp.einsum(
        "rhqp,rphd->rhqd",
        recent_weights.astype(jnp.bfloat16),
        recent_values,
        preferred_element_type=jnp.float32,
    )
    totals = lax.dynamic_update_slice_in_dim(
        totals,
        lax.dynamic_slice_in_dim(totals, suffix_start, suffix_rows, 0) + recent_totals,
        suffix_start,
        0,
    )
    numerators = lax.dynamic_update_slice_in_dim(
        numerators,
        lax.dynamic_slice_in_dim(numerators, suffix_start, suffix_rows, 0) + recent_numerators,
        suffix_start,
        0,
    )
    back_numerators, back_totals = (
        lax.all_to_all(
            numerators.reshape(seq_count, request_rows, group_width),
            "seq",
            split_axis=0,
            concat_axis=0,
            tiled=True,
        ),
        lax.all_to_all(
            totals.reshape(seq_count, request_rows, heads_here * per_kv),
            "seq",
            split_axis=0,
            concat_axis=0,
            tiled=True,
        ),
    )
    back_numerators = back_numerators.reshape(
        sub_blocks, head_groups, request_rows, heads_here * per_kv, HD
    ).sum(0)
    back_totals = back_totals.reshape(
        sub_blocks, head_groups, request_rows, heads_here * per_kv
    ).sum(0)
    attention = (
        (back_numerators / back_totals[..., None])
        .transpose(1, 0, 2, 3)
        .reshape(request_rows, NQH * HD)
    )
    return (new_cache, attention.astype(jnp.bfloat16))


def weigh(scores):
    return jnp.exp2((softcap * math.log2(math.e)) * jnp.tanh(scores * (query_scale / softcap)))


NT = (((1,), (1,)), ((), ()))
NN = (((1,), (0,)), ((), ()))


def pin(x, space=pltpu.VMEM):
    return pltpu.with_memory_space_constraint(x, space)


VMEM = pl.BlockSpec(memory_space=pltpu.VMEM)
HBM = pl.BlockSpec(memory_space=pltpu.HBM)
WIDE = 128


def turns(count):
    return [*range(count // 2, count), *range(1, count // 2), 0]


def prepare_kernel(count, core_count, prefix_length, request_rows, rates_ref, stored_assign, stored_lengths, stored_kv, *refs):
    stored, refs = refs[:4], refs[4:]
    blocks, refs = refs[:count], refs[count:]
    which_ref, live_ref, *fetched, kv_ref, cut_ref, assign_ref, lengths_ref, sems, out_sems = refs
    first_copies = [
        pltpu.make_async_copy(stored_kv, kv_ref, sems.at[4]),
        pltpu.make_async_copy(stored_assign, assign_ref, sems.at[5]),
        pltpu.make_async_copy(stored_lengths, lengths_ref, sems.at[6]),
    ]
    for copy in first_copies:
        copy.start()
    copies = [pltpu.make_async_copy(a, b, sems.at[i]) for i, (a, b) in enumerate(zip(stored, fetched))]
    for copy in copies:
        copy.start()
    place = lax.axis_index("seq")
    rows = kv_ref.shape[1]
    width = kv_ref.shape[2] // count
    first = (place * core_count + lax.axis_index("pd")) * rows
    position = (first + lax.broadcasted_iota(jnp.int32, (rows, HD), 0)) % prefix_length
    angles = position.astype(jnp.float32) * rates_ref[...]
    cosine = jnp.cos(angles)
    sine = jnp.sin(angles)
    sine = jnp.where(lax.broadcasted_iota(jnp.int32, (rows, HD), 1) < HD // 2, -sine, sine)
    for copy in first_copies:
        copy.wait()
    for slot, k in enumerate(turns(count)):
        start = jnp.bitwise_xor(place, k) * width
        for h in range(width // HD):
            columns = pl.ds(pl.multiple_of(start + h * HD, HD), HD)
            keys = kv_ref[0, :, columns].astype(jnp.float32)
            turned = pltpu.roll(keys, HD // 2, 1)
            cut = blocks[slot] if k == 0 else cut_ref.at[slot]
            cut[0, :, h * HD : (h + 1) * HD] = (keys * cosine + turned * sine).astype(jnp.bfloat16)
            cut[1, :, h * HD : (h + 1) * HD] = kv_ref[1, :, columns]
        if k:
            copies.append(pltpu.make_async_copy(cut_ref.at[slot], blocks[slot], out_sems.at[slot]))
            copies[-1].start()
    tall = which_ref.shape[0]
    which_ref[...] = jnp.broadcast_to(own_column(assign_ref, tall, request_rows, core_count), which_ref.shape)
    live_ref[...] = jnp.broadcast_to(own_column(lengths_ref, tall, request_rows, core_count), live_ref.shape)
    for copy in copies:
        copy.wait()


def own_column(values_ref, tall, request_rows, core_count):
    shape = (tall, values_ref.shape[1])
    row = lax.broadcasted_iota(jnp.int32, shape, 0) % (values_ref.shape[1] // core_count)
    wanted = (row // request_rows * core_count + lax.axis_index("pd")) * request_rows + row % request_rows
    picked = jnp.where(lax.broadcasted_iota(jnp.int32, shape, 1) == wanted, values_ref[...], 0)
    return jnp.sum(picked.astype(jnp.float32), axis=1, keepdims=True).astype(jnp.int32)


def attend_kernel(q_ref, keys_ref, values_ref, skeys_ref, svalues_ref, which_ref, live_ref, out_ref):
    seq_count, span, group_width = q_ref.shape
    requests = seq_count * span
    per_kv = NQH // KVH
    heads_here = keys_ref.shape[2] // HD
    length = keys_ref.shape[1] // NPFX
    slots = skeys_ref.shape[3]
    queries = q_ref[...].reshape(requests, group_width)
    column = lax.broadcasted_iota(jnp.int32, (span * per_kv, span * slots), 1)
    low = lax.broadcasted_iota(jnp.int32, (span * per_kv, span * slots), 0) % span * slots
    for h in range(heads_here):
        columns = slice(h * HD, (h + 1) * HD)
        query = jnp.concatenate(
            [queries[:, (h * per_kv + j) * HD : (h * per_kv + j + 1) * HD] for j in range(per_kv)], axis=0
        )
        query32 = query.astype(jnp.float32)
        picked = [
            [slice(j * requests + b * span, j * requests + (b + 1) * span) for j in range(per_kv)]
            for b in range(seq_count)
        ]
        added, more = [], []
        for b in range(seq_count):
            part = jnp.concatenate([query32[rows] for rows in picked[b]], axis=0).astype(jnp.bfloat16)
            skeys = skeys_ref[0, 0, b * span : (b + 1) * span, :, columns].reshape(span * slots, HD)
            svalues = svalues_ref[0, 0, b * span : (b + 1) * span, :, columns].reshape(span * slots, HD)
            recent = weigh(lax.dot_general(part, skeys, NT, preferred_element_type=jnp.float32))
            live = jnp.concatenate([live_ref[rows, :1] for rows in picked[b]], axis=0)
            recent = jnp.where((column >= low) & (column < low + live), recent, 0.0)
            more.append(jnp.sum(recent, axis=1, keepdims=True))
            added.append(lax.dot_general(recent.astype(jnp.bfloat16), svalues, NN, preferred_element_type=jnp.float32))
        scores = lax.dot_general(query, keys_ref[0, :length, columns], NT, preferred_element_type=jnp.float32)
        for p in range(1, NPFX):
            other = lax.dot_general(
                query, keys_ref[0, p * length : (p + 1) * length, columns], NT, preferred_element_type=jnp.float32
            )
            scores = jnp.where(which_ref[:, :1] == p, other, scores)
        weights = weigh(scores)
        total = jnp.sum(weights, axis=1, keepdims=True)
        rounded = weights.astype(jnp.bfloat16)
        numerator = jnp.dot(rounded, values_ref[0, :length, columns], preferred_element_type=jnp.float32)
        for p in range(1, NPFX):
            other = jnp.dot(
                rounded, values_ref[0, p * length : (p + 1) * length, columns], preferred_element_type=jnp.float32
            )
            numerator = jnp.where(which_ref[...] == p, other, numerator)

        def regroup(parts):
            return jnp.concatenate(
                [parts[b][j * span : (j + 1) * span] for j in range(per_kv) for b in range(seq_count)], axis=0
            )

        result = (numerator + regroup(added)) * (1.0 / (total + regroup(more)))
        for j in range(per_kv):
            head = h * per_kv + j
            out_ref[:, :, head * HD : (head + 1) * HD] = result[j * requests : (j + 1) * requests].reshape(
                seq_count, span, HD
            ).astype(jnp.bfloat16)


def finish_kernel(count, back_ref, *refs):
    *pieces, cache_ref, attention_ref, sems = refs
    place = lax.axis_index("seq")
    copies = [
        pltpu.make_async_copy(piece, cache_ref.at[:, 0, jnp.bitwise_xor(place, k)], sems.at[k])
        for k, piece in zip(turns(count), pieces)
    ]
    for copy in copies:
        copy.start()
    width = back_ref.shape[2]
    for s in range(count):
        attention_ref[:, s * width : (s + 1) * width] = back_ref[s]
    for copy in copies:
        copy.wait()


def local(new_kv, old_keys, old_values, suffix_keys, suffix_values, queries, lengths, assign):
    seq_count = lax.axis_size("seq")
    core_count = lax.axis_size("pd")
    if seq_count > KVH or seq_count & (seq_count - 1):
        return general(new_kv, old_keys, old_values, suffix_keys, suffix_values, queries, lengths, assign)
    request_rows = queries.shape[0]
    prefix_rows = new_kv.shape[1]
    group_width = queries.shape[1] // seq_count
    width = new_kv.shape[2] // seq_count
    tall = NQH // KVH * seq_count * request_rows
    prefix_length = prefix_rows * seq_count * core_count // NPFX
    rates = (10000.0 ** (-2.0 * (np.arange(HD) % (HD // 2)) / HD)).astype(np.float32)
    asked = lax.all_to_all(
        queries.reshape(request_rows, seq_count, group_width).transpose(1, 0, 2), "seq", 0, 0, tiled=True
    )
    stored = (old_keys, old_values, suffix_keys, suffix_values)
    block = pltpu.HBM((2, prefix_rows, width), jnp.bfloat16)
    mine = jax.ShapeDtypeStruct((2, prefix_rows, width), jnp.bfloat16)
    column = jax.ShapeDtypeStruct((tall, WIDE), jnp.int32)
    prepared = pl.pallas_call(
        functools.partial(prepare_kernel, seq_count, core_count, prefix_length, request_rows),
        out_shape=[block] * (seq_count - 1) + [mine] + [column] * 2 + [jax.ShapeDtypeStruct(x.shape, x.dtype) for x in stored],
        in_specs=[VMEM] + [HBM] * 7,
        out_specs=[HBM] * (seq_count - 1) + [VMEM] * 7,
        scratch_shapes=[
            pltpu.VMEM(new_kv.shape, jnp.bfloat16),
            pltpu.VMEM((seq_count - 1, 2, prefix_rows, width), jnp.bfloat16),
            pltpu.VMEM((1, assign.shape[0]), jnp.int32),
            pltpu.VMEM((1, assign.shape[0]), jnp.int32),
            pltpu.SemaphoreType.DMA((7,)),
            pltpu.SemaphoreType.DMA((seq_count - 1,)),
        ],
        cost_estimate=pl.CostEstimate(flops=1000, bytes_accessed=1000, transcendentals=0),
        compiler_params=pltpu.CompilerParams(vmem_limit_bytes=24 * 2**20),
    )(
        jnp.asarray(rates).reshape(1, HD),
        *(pin(x, pltpu.HBM) for x in (assign.reshape(1, -1), lengths.reshape(1, -1), new_kv, *stored)),
    )
    blocks, (which, live, *fetched) = prepared[:seq_count], prepared[seq_count:]
    pieces = [
        lax.ppermute(block, "seq", [(i, i ^ k) for i in range(seq_count)]) if k else block
        for k, block in zip(turns(seq_count), blocks)
    ]
    attended = pl.pallas_call(
        attend_kernel,
        out_shape=jax.ShapeDtypeStruct((seq_count, request_rows, group_width), jnp.bfloat16),
        in_specs=[VMEM] * 7,
        out_specs=VMEM,
        compiler_params=pltpu.CompilerParams(vmem_limit_bytes=16 * 2**20),
        cost_estimate=pl.CostEstimate(flops=2**20, bytes_accessed=2**20, transcendentals=2**10),
    )(pin(asked), *(pin(x) for x in fetched), pin(which), pin(live))
    back = lax.all_to_all(attended, "seq", 0, 0, tiled=True)
    return tuple(
        pl.pallas_call(
            functools.partial(finish_kernel, seq_count),
            out_shape=(
                jax.ShapeDtypeStruct((2, 1, seq_count, prefix_rows, width), jnp.bfloat16),
                jax.ShapeDtypeStruct((request_rows, NQH * HD), jnp.bfloat16),
            ),
            in_specs=[VMEM] * (seq_count + 1),
            out_specs=(HBM, VMEM),
            scratch_shapes=[pltpu.SemaphoreType.DMA((seq_count,))],
            cost_estimate=pl.CostEstimate(flops=0, bytes_accessed=2**20, transcendentals=0),
        )(pin(back), *(pin(piece) for piece in pieces))
    )


def solution(mesh):
    return jax.shard_map(
        local,
        mesh=mesh,
        in_specs=(
            P("grp", ("seq", "pd"), None),
            P("seq", "grp", None),
            P("seq", "grp", None),
            P("pd", "seq", "grp", None, None),
            P("pd", "seq", "grp", None, None),
            P(("seq", "pd"), "grp"),
            P("grp"),
            P("grp"),
        ),
        out_specs=(P(None, "seq", "grp", "pd", None), P(("seq", "pd"), "grp")),
        check_vma=False,
    )
```

```python
import functools
import math

import jax
import jax.numpy as jnp
import numpy as np
from jax import lax
from jax.experimental import pallas as pl
from jax.experimental.pallas import tpu as pltpu
from jax.sharding import PartitionSpec as P

HD = 128
KVH = 16
NQH = 32
NPFX = 2


softcap = 50.0
query_scale = 1.0 / 12.0


def rotary(key_rows, positions):
    head_width = key_rows.shape[-1]
    halfway = head_width // 2
    inverse = 10000.0 ** (-2.0 * jnp.arange(halfway).astype(jnp.float32) / head_width)
    angles = positions.astype(jnp.float32)[:, None] * inverse[None, :]
    angles = jnp.concatenate([angles, angles], axis=1)
    values = key_rows.astype(jnp.float32)
    turned = jnp.concatenate([-values[..., halfway:], values[..., :halfway]], axis=-1)
    return values * jnp.cos(angles)[:, None, :] + turned * jnp.sin(angles)[:, None, :]


def capped(scores):
    return softcap * jnp.tanh(scores * query_scale / softcap)


def general(new_kv, old_keys, old_values, suffix_keys, suffix_values, queries, lengths, assign):
    seq_count = lax.axis_size("seq")
    core_count = lax.axis_size("pd")
    seq_place = lax.axis_index("seq")
    core_place = lax.axis_index("pd")
    per_kv = NQH // KVH
    sub_blocks = max(seq_count // KVH, 1)
    heads_here = max(KVH // seq_count, 1)
    head_groups = KVH // heads_here
    prefix_rows = new_kv.shape[1]
    request_rows = queries.shape[0]
    prefix_length = prefix_rows * seq_count * core_count // NPFX
    group_width = heads_here * per_kv * HD
    positions = (
        (seq_place * core_count + core_place) * prefix_rows
        + jnp.arange(prefix_rows, dtype=jnp.int32)
    ) % prefix_length
    rotated = rotary(new_kv[0].reshape(prefix_rows, KVH, HD), positions).astype(jnp.bfloat16)
    rotated = rotated.reshape(prefix_rows, KVH * HD)
    outgoing = jnp.stack([rotated, new_kv[1]]).reshape(
        2, prefix_rows // sub_blocks, seq_count, heads_here * HD
    )
    arrived = lax.all_to_all(outgoing, "seq", split_axis=2, concat_axis=1, tiled=True)
    new_cache = arrived.reshape(2, 1, seq_count, prefix_rows // sub_blocks, heads_here * HD)
    head_group = seq_place % head_groups
    token_block = seq_place // head_groups
    half_rows = seq_count * request_rows
    gathered = lax.all_gather(queries, "seq", axis=0, tiled=True)
    own_queries = lax.dynamic_slice_in_dim(gathered, head_group * group_width, group_width, 1)
    query_blocks = own_queries.reshape(half_rows, heads_here, per_kv, HD)
    own_assign = lax.dynamic_index_in_dim(
        assign.reshape(seq_count, core_count, request_rows), core_place, 1, keepdims=False
    ).reshape(half_rows)
    own_lengths = lax.dynamic_index_in_dim(
        lengths.reshape(seq_count, core_count, request_rows), core_place, 1, keepdims=False
    ).reshape(half_rows)
    prefix_keys = old_keys[0].reshape(-1, heads_here, HD)
    prefix_values = old_values[0].reshape(-1, heads_here, HD)
    token_count = prefix_keys.shape[0]
    token_prefix = (
        jnp.arange(token_count, dtype=jnp.int32) * sub_blocks + token_block
    ) // prefix_length
    block_rows = math.gcd(half_rows, 256)

    def prefix_block(block_index):
        row_start = block_index * block_rows
        query_part = lax.dynamic_slice_in_dim(query_blocks, row_start, block_rows, 0)
        assign_part = lax.dynamic_slice_in_dim(own_assign, row_start, block_rows, 0)
        scores = capped(
            jnp.einsum(
                "rhqd,thd->rhqt", query_part, prefix_keys, preferred_element_type=jnp.float32
            )
        )
        allowed = (assign_part[:, None] == token_prefix[None, :])[:, None, None, :]
        weights = jnp.where(allowed, jnp.exp(scores), 0.0)
        totals = jnp.sum(weights, axis=-1)
        numerators = jnp.einsum(
            "rhqt,thd->rhqd",
            weights.astype(jnp.bfloat16),
            prefix_values,
            preferred_element_type=jnp.float32,
        )
        return (totals, numerators)

    totals, numerators = lax.map(prefix_block, jnp.arange(half_rows // block_rows, dtype=jnp.int32))
    totals = totals.reshape(half_rows, heads_here, per_kv)
    numerators = numerators.reshape(half_rows, heads_here, per_kv, HD)
    suffix_rows = head_groups * request_rows
    suffix_start = token_block * suffix_rows
    suffix_query = lax.dynamic_slice_in_dim(query_blocks, suffix_start, suffix_rows, 0)
    suffix_length = lax.dynamic_slice_in_dim(own_lengths, suffix_start, suffix_rows, 0)
    recent_keys = suffix_keys[0, 0].reshape(suffix_rows, -1, heads_here, HD)
    recent_values = suffix_values[0, 0].reshape(suffix_rows, -1, heads_here, HD)
    recent_scores = capped(
        jnp.einsum("rhqd,rphd->rhqp", suffix_query, recent_keys, preferred_element_type=jnp.float32)
    )
    live_slots = jnp.arange(recent_keys.shape[1], dtype=jnp.int32)[None, :] < suffix_length[:, None]
    recent_weights = jnp.where(live_slots[:, None, None, :], jnp.exp(recent_scores), 0.0)
    recent_totals = jnp.sum(recent_weights, axis=-1)
    recent_numerators = jnp.einsum(
        "rhqp,rphd->rhqd",
        recent_weights.astype(jnp.bfloat16),
        recent_values,
        preferred_element_type=jnp.float32,
    )
    totals = lax.dynamic_update_slice_in_dim(
        totals,
        lax.dynamic_slice_in_dim(totals, suffix_start, suffix_rows, 0) + recent_totals,
        suffix_start,
        0,
    )
    numerators = lax.dynamic_update_slice_in_dim(
        numerators,
        lax.dynamic_slice_in_dim(numerators, suffix_start, suffix_rows, 0) + recent_numerators,
        suffix_start,
        0,
    )
    back_numerators, back_totals = (
        lax.all_to_all(
            numerators.reshape(seq_count, request_rows, group_width),
            "seq",
            split_axis=0,
            concat_axis=0,
            tiled=True,
        ),
        lax.all_to_all(
            totals.reshape(seq_count, request_rows, heads_here * per_kv),
            "seq",
            split_axis=0,
            concat_axis=0,
            tiled=True,
        ),
    )
    back_numerators = back_numerators.reshape(
        sub_blocks, head_groups, request_rows, heads_here * per_kv, HD
    ).sum(0)
    back_totals = back_totals.reshape(
        sub_blocks, head_groups, request_rows, heads_here * per_kv
    ).sum(0)
    attention = (
        (back_numerators / back_totals[..., None])
        .transpose(1, 0, 2, 3)
        .reshape(request_rows, NQH * HD)
    )
    return (new_cache, attention.astype(jnp.bfloat16))


def weigh(scores):
    return jnp.exp2((softcap * math.log2(math.e)) * jnp.tanh(scores * (query_scale / softcap)))


NT = (((1,), (1,)), ((), ()))
NN = (((1,), (0,)), ((), ()))


def pin(x, space=pltpu.VMEM):
    return pltpu.with_memory_space_constraint(x, space)


VMEM = pl.BlockSpec(memory_space=pltpu.VMEM)
HBM = pl.BlockSpec(memory_space=pltpu.HBM)
WIDE = 128


def turns(count):
    return [*range(count // 2, count), *range(1, count // 2), 0]


def prepare_kernel(count, core_count, prefix_length, request_rows, stored_rates, stored_assign, stored_lengths, stored_kv, *refs):
    stored, refs = refs[:4], refs[4:]
    blocks, refs = refs[:count], refs[count:]
    which_ref, live_ref, *fetched, rates_ref, kv_ref, cut_ref, assign_ref, lengths_ref, sems, out_sems = refs
    first_copies = [
        pltpu.make_async_copy(stored_rates, rates_ref, sems.at[7]),
        pltpu.make_async_copy(stored_kv, kv_ref, sems.at[4]),
        pltpu.make_async_copy(stored_assign, assign_ref, sems.at[5]),
        pltpu.make_async_copy(stored_lengths, lengths_ref, sems.at[6]),
    ]
    for copy in first_copies:
        copy.start()
    copies = [pltpu.make_async_copy(a, b, sems.at[i]) for i, (a, b) in enumerate(zip(stored, fetched))]
    for copy in copies:
        copy.start()
    first_copies[0].wait()
    place = lax.axis_index("seq")
    rows = kv_ref.shape[1]
    width = kv_ref.shape[2] // count
    first = (place * core_count + lax.axis_index("pd")) * rows
    position = (first + lax.broadcasted_iota(jnp.int32, (rows, HD), 0)) % prefix_length
    angles = position.astype(jnp.float32) * rates_ref[...]
    cosine = jnp.cos(angles)
    sine = jnp.sin(angles)
    sine = jnp.where(lax.broadcasted_iota(jnp.int32, (rows, HD), 1) < HD // 2, -sine, sine)
    for copy in first_copies[1:]:
        copy.wait()
    for slot, k in enumerate(turns(count)):
        start = jnp.bitwise_xor(place, k) * width
        for h in range(width // HD):
            columns = pl.ds(pl.multiple_of(start + h * HD, HD), HD)
            keys = kv_ref[0, :, columns].astype(jnp.float32)
            turned = pltpu.roll(keys, HD // 2, 1)
            cut = blocks[slot] if k == 0 else cut_ref.at[slot]
            cut[0, :, h * HD : (h + 1) * HD] = (keys * cosine + turned * sine).astype(jnp.bfloat16)
            cut[1, :, h * HD : (h + 1) * HD] = kv_ref[1, :, columns]
        if k:
            copies.append(pltpu.make_async_copy(cut_ref.at[slot], blocks[slot], out_sems.at[slot]))
            copies[-1].start()
    tall = which_ref.shape[0]
    which_ref[...] = jnp.broadcast_to(own_column(assign_ref, tall, request_rows, core_count), which_ref.shape)
    live_ref[...] = jnp.broadcast_to(own_column(lengths_ref, tall, request_rows, core_count), live_ref.shape)
    for copy in copies:
        copy.wait()


def own_column(values_ref, tall, request_rows, core_count):
    shape = (tall, values_ref.shape[1])
    row = lax.broadcasted_iota(jnp.int32, shape, 0) % (values_ref.shape[1] // core_count)
    wanted = (row // request_rows * core_count + lax.axis_index("pd")) * request_rows + row % request_rows
    picked = jnp.where(lax.broadcasted_iota(jnp.int32, shape, 1) == wanted, values_ref[...], 0)
    return jnp.sum(picked.astype(jnp.float32), axis=1, keepdims=True).astype(jnp.int32)


def attend_kernel(q_ref, keys_ref, values_ref, skeys_ref, svalues_ref, which_ref, live_ref, out_ref):
    seq_count, span, group_width = q_ref.shape
    requests = seq_count * span
    per_kv = NQH // KVH
    width = keys_ref.shape[2]
    heads_here = width // HD
    length = keys_ref.shape[1] // NPFX
    slots = skeys_ref.shape[3]
    queries = q_ref[...].reshape(requests, group_width)
    heads = [(h, j) for h in range(heads_here) for j in range(per_kv)]
    query = {(h, j): queries[:, (h * per_kv + j) * HD : (h * per_kv + j + 1) * HD] for h, j in heads}
    query32 = {key: value.astype(jnp.float32) for key, value in query.items()}
    blank = jnp.zeros((span, HD), jnp.float32)
    tall = span * len(heads)
    column = lax.broadcasted_iota(jnp.int32, (tall, span * slots), 1)
    low = lax.broadcasted_iota(jnp.int32, (tall, span * slots), 0) % span * slots
    added, more, found = {}, {}, []
    blocks = [slice(b * span, (b + 1) * span) for b in range(seq_count)]
    for rows in blocks:
        part = jnp.concatenate(
            [
                jnp.concatenate([query32[h, j][rows] if g == h else blank for g in range(heads_here)], axis=1)
                for h, j in heads
            ],
            axis=0,
        ).astype(jnp.bfloat16)
        skeys = skeys_ref[0, 0, rows].reshape(span * slots, width)
        found.append(lax.dot_general(part, skeys, NT, preferred_element_type=jnp.float32))
    for b, rows in enumerate(blocks):
        live = jnp.concatenate([live_ref[rows, :1]] * len(heads), axis=0)
        found[b] = jnp.where((column >= low) & (column < low + live), weigh(found[b]), 0.0)
    for b, rows in enumerate(blocks):
        svalues = svalues_ref[0, 0, rows].reshape(span * slots, width)
        sums = jnp.sum(found[b], axis=1, keepdims=True)
        products = jnp.dot(found[b].astype(jnp.bfloat16), svalues, preferred_element_type=jnp.float32)
        for i, (h, j) in enumerate(heads):
            more[h, j, b] = sums[i * span : (i + 1) * span]
            added[h, j, b] = products[i * span : (i + 1) * span, h * HD : (h + 1) * HD]
    for h in range(heads_here):
        columns = slice(h * HD, (h + 1) * HD)
        stacked = jnp.concatenate([query[h, j] for j in range(per_kv)], axis=0)
        scores = lax.dot_general(stacked, keys_ref[0, :length, columns], NT, preferred_element_type=jnp.float32)
        for p in range(1, NPFX):
            other = lax.dot_general(
                stacked, keys_ref[0, p * length : (p + 1) * length, columns], NT, preferred_element_type=jnp.float32
            )
            scores = jnp.where(which_ref[:, :1] == p, other, scores)
        weights = weigh(scores)
        total = jnp.sum(weights, axis=1, keepdims=True)
        rounded = weights.astype(jnp.bfloat16)
        numerator = jnp.dot(rounded, values_ref[0, :length, columns], preferred_element_type=jnp.float32)
        for p in range(1, NPFX):
            other = jnp.dot(
                rounded, values_ref[0, p * length : (p + 1) * length, columns], preferred_element_type=jnp.float32
            )
            numerator = jnp.where(which_ref[...] == p, other, numerator)

        def regroup(parts):
            return jnp.concatenate([parts[h, j, b] for j in range(per_kv) for b in range(seq_count)], axis=0)

        result = (numerator + regroup(added)) * (1.0 / (total + regroup(more)))
        for j in range(per_kv):
            head = h * per_kv + j
            out_ref[:, :, head * HD : (head + 1) * HD] = result[j * requests : (j + 1) * requests].reshape(
                seq_count, span, HD
            ).astype(jnp.bfloat16)


def finish_kernel(count, back_ref, *refs):
    *pieces, cache_ref, attention_ref, sems = refs
    place = lax.axis_index("seq")
    copies = [
        pltpu.make_async_copy(piece, cache_ref.at[:, 0, jnp.bitwise_xor(place, k)], sems.at[k])
        for k, piece in zip(turns(count), pieces)
    ]
    for copy in copies:
        copy.start()
    width = back_ref.shape[2]
    for s in range(count):
        attention_ref[:, s * width : (s + 1) * width] = back_ref[s]
    for copy in copies:
        copy.wait()


def local(new_kv, old_keys, old_values, suffix_keys, suffix_values, queries, lengths, assign):
    seq_count = lax.axis_size("seq")
    core_count = lax.axis_size("pd")
    if seq_count > KVH or seq_count & (seq_count - 1):
        return general(new_kv, old_keys, old_values, suffix_keys, suffix_values, queries, lengths, assign)
    request_rows = queries.shape[0]
    prefix_rows = new_kv.shape[1]
    group_width = queries.shape[1] // seq_count
    width = new_kv.shape[2] // seq_count
    tall = NQH // KVH * seq_count * request_rows
    prefix_length = prefix_rows * seq_count * core_count // NPFX
    rates = (10000.0 ** (-2.0 * (np.arange(HD) % (HD // 2)) / HD)).astype(np.float32)
    asked = lax.all_to_all(
        queries.reshape(request_rows, seq_count, group_width).transpose(1, 0, 2), "seq", 0, 0, tiled=True
    )
    stored = (old_keys, old_values, suffix_keys, suffix_values)
    block = pltpu.HBM((2, prefix_rows, width), jnp.bfloat16)
    mine = pltpu.VMEM((2, prefix_rows, width), jnp.bfloat16)
    column = pltpu.VMEM((tall, WIDE), jnp.int32)
    prepared = pl.pallas_call(
        functools.partial(prepare_kernel, seq_count, core_count, prefix_length, request_rows),
        out_shape=[block] * (seq_count - 1) + [mine] + [column] * 2 + [pltpu.VMEM(x.shape, x.dtype) for x in stored],
        in_specs=[HBM] * 8,
        out_specs=[HBM] * (seq_count - 1) + [VMEM] * 7,
        scratch_shapes=[
            pltpu.VMEM((1, HD), jnp.float32),
            pltpu.VMEM(new_kv.shape, jnp.bfloat16),
            pltpu.VMEM((seq_count - 1, 2, prefix_rows, width), jnp.bfloat16),
            pltpu.VMEM((1, assign.shape[0]), jnp.int32),
            pltpu.VMEM((1, assign.shape[0]), jnp.int32),
            pltpu.SemaphoreType.DMA((8,)),
            pltpu.SemaphoreType.DMA((seq_count - 1,)),
        ],
        cost_estimate=pl.CostEstimate(flops=1000, bytes_accessed=1000, transcendentals=0),
        compiler_params=pltpu.CompilerParams(vmem_limit_bytes=24 * 2**20),
    )(
        *(pin(x, pltpu.HBM) for x in (jnp.asarray(rates).reshape(1, HD), assign.reshape(1, -1), lengths.reshape(1, -1), new_kv, *stored)),
    )
    blocks, (which, live, *fetched) = prepared[:seq_count], prepared[seq_count:]
    pieces = [
        lax.ppermute(block, "seq", [(i, i ^ k) for i in range(seq_count)]) if k else block
        for k, block in zip(turns(seq_count), blocks)
    ]
    attended = pl.pallas_call(
        attend_kernel,
        out_shape=pltpu.VMEM((seq_count, request_rows, group_width), jnp.bfloat16),
        in_specs=[VMEM] * 7,
        out_specs=VMEM,
        compiler_params=pltpu.CompilerParams(vmem_limit_bytes=16 * 2**20),
        cost_estimate=pl.CostEstimate(flops=2**20, bytes_accessed=2**20, transcendentals=2**10),
    )(pin(asked), *(pin(x) for x in fetched), pin(which), pin(live))
    back = lax.all_to_all(attended, "seq", 0, 0, tiled=True)
    return tuple(
        pl.pallas_call(
            functools.partial(finish_kernel, seq_count),
            out_shape=(
                jax.ShapeDtypeStruct((2, 1, seq_count, prefix_rows, width), jnp.bfloat16),
                jax.ShapeDtypeStruct((request_rows, NQH * HD), jnp.bfloat16),
            ),
            in_specs=[VMEM] * (seq_count + 1),
            out_specs=(HBM, VMEM),
            scratch_shapes=[pltpu.SemaphoreType.DMA((seq_count,))],
            cost_estimate=pl.CostEstimate(flops=0, bytes_accessed=2**20, transcendentals=0),
        )(pin(back), *(pin(piece) for piece in pieces))
    )


def solution(mesh):
    return jax.shard_map(
        local,
        mesh=mesh,
        in_specs=(
            P("grp", ("seq", "pd"), None),
            P("seq", "grp", None),
            P("seq", "grp", None),
            P("pd", "seq", "grp", None, None),
            P("pd", "seq", "grp", None, None),
            P(("seq", "pd"), "grp"),
            P("grp"),
            P("grp"),
        ),
        out_specs=(P(None, "seq", "grp", "pd", None), P(("seq", "pd"), "grp")),
        check_vma=False,
    )
```

```python
import functools
import math

import jax
import jax.numpy as jnp
import numpy as np
from jax import lax
from jax.experimental import pallas as pl
from jax.experimental.pallas import tpu as pltpu
from jax.sharding import PartitionSpec as P

HD = 128
KVH = 16
NQH = 32
NPFX = 2


softcap = 50.0
query_scale = 1.0 / 12.0


def rotary(key_rows, positions):
    head_width = key_rows.shape[-1]
    halfway = head_width // 2
    inverse = 10000.0 ** (-2.0 * jnp.arange(halfway).astype(jnp.float32) / head_width)
    angles = positions.astype(jnp.float32)[:, None] * inverse[None, :]
    angles = jnp.concatenate([angles, angles], axis=1)
    values = key_rows.astype(jnp.float32)
    turned = jnp.concatenate([-values[..., halfway:], values[..., :halfway]], axis=-1)
    return values * jnp.cos(angles)[:, None, :] + turned * jnp.sin(angles)[:, None, :]


def capped(scores):
    return softcap * jnp.tanh(scores * query_scale / softcap)


def general(new_kv, old_keys, old_values, suffix_keys, suffix_values, queries, lengths, assign):
    seq_count = lax.axis_size("seq")
    core_count = lax.axis_size("pd")
    seq_place = lax.axis_index("seq")
    core_place = lax.axis_index("pd")
    per_kv = NQH // KVH
    sub_blocks = max(seq_count // KVH, 1)
    heads_here = max(KVH // seq_count, 1)
    head_groups = KVH // heads_here
    prefix_rows = new_kv.shape[1]
    request_rows = queries.shape[0]
    prefix_length = prefix_rows * seq_count * core_count // NPFX
    group_width = heads_here * per_kv * HD
    positions = (
        (seq_place * core_count + core_place) * prefix_rows
        + jnp.arange(prefix_rows, dtype=jnp.int32)
    ) % prefix_length
    rotated = rotary(new_kv[0].reshape(prefix_rows, KVH, HD), positions).astype(jnp.bfloat16)
    rotated = rotated.reshape(prefix_rows, KVH * HD)
    outgoing = jnp.stack([rotated, new_kv[1]]).reshape(
        2, prefix_rows // sub_blocks, seq_count, heads_here * HD
    )
    arrived = lax.all_to_all(outgoing, "seq", split_axis=2, concat_axis=1, tiled=True)
    new_cache = arrived.reshape(2, 1, seq_count, prefix_rows // sub_blocks, heads_here * HD)
    head_group = seq_place % head_groups
    token_block = seq_place // head_groups
    half_rows = seq_count * request_rows
    gathered = lax.all_gather(queries, "seq", axis=0, tiled=True)
    own_queries = lax.dynamic_slice_in_dim(gathered, head_group * group_width, group_width, 1)
    query_blocks = own_queries.reshape(half_rows, heads_here, per_kv, HD)
    own_assign = lax.dynamic_index_in_dim(
        assign.reshape(seq_count, core_count, request_rows), core_place, 1, keepdims=False
    ).reshape(half_rows)
    own_lengths = lax.dynamic_index_in_dim(
        lengths.reshape(seq_count, core_count, request_rows), core_place, 1, keepdims=False
    ).reshape(half_rows)
    prefix_keys = old_keys[0].reshape(-1, heads_here, HD)
    prefix_values = old_values[0].reshape(-1, heads_here, HD)
    token_count = prefix_keys.shape[0]
    token_prefix = (
        jnp.arange(token_count, dtype=jnp.int32) * sub_blocks + token_block
    ) // prefix_length
    block_rows = math.gcd(half_rows, 256)

    def prefix_block(block_index):
        row_start = block_index * block_rows
        query_part = lax.dynamic_slice_in_dim(query_blocks, row_start, block_rows, 0)
        assign_part = lax.dynamic_slice_in_dim(own_assign, row_start, block_rows, 0)
        scores = capped(
            jnp.einsum(
                "rhqd,thd->rhqt", query_part, prefix_keys, preferred_element_type=jnp.float32
            )
        )
        allowed = (assign_part[:, None] == token_prefix[None, :])[:, None, None, :]
        weights = jnp.where(allowed, jnp.exp(scores), 0.0)
        totals = jnp.sum(weights, axis=-1)
        numerators = jnp.einsum(
            "rhqt,thd->rhqd",
            weights.astype(jnp.bfloat16),
            prefix_values,
            preferred_element_type=jnp.float32,
        )
        return (totals, numerators)

    totals, numerators = lax.map(prefix_block, jnp.arange(half_rows // block_rows, dtype=jnp.int32))
    totals = totals.reshape(half_rows, heads_here, per_kv)
    numerators = numerators.reshape(half_rows, heads_here, per_kv, HD)
    suffix_rows = head_groups * request_rows
    suffix_start = token_block * suffix_rows
    suffix_query = lax.dynamic_slice_in_dim(query_blocks, suffix_start, suffix_rows, 0)
    suffix_length = lax.dynamic_slice_in_dim(own_lengths, suffix_start, suffix_rows, 0)
    recent_keys = suffix_keys[0, 0].reshape(suffix_rows, -1, heads_here, HD)
    recent_values = suffix_values[0, 0].reshape(suffix_rows, -1, heads_here, HD)
    recent_scores = capped(
        jnp.einsum("rhqd,rphd->rhqp", suffix_query, recent_keys, preferred_element_type=jnp.float32)
    )
    live_slots = jnp.arange(recent_keys.shape[1], dtype=jnp.int32)[None, :] < suffix_length[:, None]
    recent_weights = jnp.where(live_slots[:, None, None, :], jnp.exp(recent_scores), 0.0)
    recent_totals = jnp.sum(recent_weights, axis=-1)
    recent_numerators = jnp.einsum(
        "rhqp,rphd->rhqd",
        recent_weights.astype(jnp.bfloat16),
        recent_values,
        preferred_element_type=jnp.float32,
    )
    totals = lax.dynamic_update_slice_in_dim(
        totals,
        lax.dynamic_slice_in_dim(totals, suffix_start, suffix_rows, 0) + recent_totals,
        suffix_start,
        0,
    )
    numerators = lax.dynamic_update_slice_in_dim(
        numerators,
        lax.dynamic_slice_in_dim(numerators, suffix_start, suffix_rows, 0) + recent_numerators,
        suffix_start,
        0,
    )
    back_numerators, back_totals = (
        lax.all_to_all(
            numerators.reshape(seq_count, request_rows, group_width),
            "seq",
            split_axis=0,
            concat_axis=0,
            tiled=True,
        ),
        lax.all_to_all(
            totals.reshape(seq_count, request_rows, heads_here * per_kv),
            "seq",
            split_axis=0,
            concat_axis=0,
            tiled=True,
        ),
    )
    back_numerators = back_numerators.reshape(
        sub_blocks, head_groups, request_rows, heads_here * per_kv, HD
    ).sum(0)
    back_totals = back_totals.reshape(
        sub_blocks, head_groups, request_rows, heads_here * per_kv
    ).sum(0)
    attention = (
        (back_numerators / back_totals[..., None])
        .transpose(1, 0, 2, 3)
        .reshape(request_rows, NQH * HD)
    )
    return (new_cache, attention.astype(jnp.bfloat16))


def weigh(scores):
    return jnp.exp2((softcap * math.log2(math.e)) * jnp.tanh(scores * (query_scale / softcap)))


NT = (((1,), (1,)), ((), ()))
NN = (((1,), (0,)), ((), ()))


def pin(x, space=pltpu.VMEM):
    return pltpu.with_memory_space_constraint(x, space)


VMEM = pl.BlockSpec(memory_space=pltpu.VMEM)
HBM = pl.BlockSpec(memory_space=pltpu.HBM)
WIDE = 128


def own_column(values_ref, tall, request_rows, core_count):
    shape = (tall, values_ref.shape[1])
    row = lax.broadcasted_iota(jnp.int32, shape, 0) % (values_ref.shape[1] // core_count)
    wanted = (row // request_rows * core_count + lax.axis_index("pd")) * request_rows + row % request_rows
    picked = jnp.where(lax.broadcasted_iota(jnp.int32, shape, 1) == wanted, values_ref[...], 0)
    return jnp.sum(picked.astype(jnp.float32), axis=1, keepdims=True).astype(jnp.int32)


def prepare_kernel(count, core_count, prefix_length, request_rows, riding, *refs):
    (stored_rates, stored_assign, stored_lengths, stored_kv), stored, refs = refs[:4], refs[4:7], refs[7:]
    own_ref, *pieces = refs[: count // 2]
    which_ref, live_ref, ride_ref, *fetched = refs[count // 2 : count // 2 + 6]
    rates_ref, assign_ref, lengths_ref, kv_ref, cut_ref, sems, out_sems = refs[count // 2 + 6 :]
    first_copies = [
        pltpu.make_async_copy(a, b, sems.at[i])
        for i, (a, b) in enumerate(
            (
                (stored_rates, rates_ref),
                (stored_kv, kv_ref),
                (stored_assign, assign_ref),
                (stored_lengths, lengths_ref),
            )
        )
    ]
    copies = [pltpu.make_async_copy(a, b, sems.at[4 + i]) for i, (a, b) in enumerate(zip(stored, fetched))]
    for copy in first_copies + copies:
        copy.start()
    first_copies[0].wait()
    place = lax.axis_index("seq")
    rows = kv_ref.shape[1]
    width = kv_ref.shape[2] // count
    first = (place * core_count + lax.axis_index("pd")) * rows
    position = (first + lax.broadcasted_iota(jnp.int32, (rows, HD), 0)) % prefix_length
    angles = position.astype(jnp.float32) * rates_ref[...]
    cosine = jnp.cos(angles)
    sine = jnp.sin(angles)
    sine = jnp.where(lax.broadcasted_iota(jnp.int32, (rows, HD), 1) < HD // 2, -sine, sine)
    for copy in first_copies[1:]:
        copy.wait()
    for j in reversed(range(count // 2)):
        cut = cut_ref.at[j - 1] if j else own_ref
        for d in range(2):
            start = jnp.bitwise_xor(place, 2 * j + d) * width
            for h in range(width // HD):
                columns = pl.ds(pl.multiple_of(start + h * HD, HD), HD)
                keys = kv_ref[0, :, columns].astype(jnp.float32)
                turned = pltpu.roll(keys, HD // 2, 1)
                cut[d, :rows, h * HD : (h + 1) * HD] = (keys * cosine + turned * sine).astype(jnp.bfloat16)
                cut[d, rows:, h * HD : (h + 1) * HD] = kv_ref[1, : rows - riding, columns]
        if j:
            copies.append(pltpu.make_async_copy(cut, pieces[j - 1], out_sems.at[j - 1]))
            copies[-1].start()
    for s in range(count):
        ride_ref[s] = kv_ref[1, rows - riding :, s * width : (s + 1) * width]
    tall = which_ref.shape[0]
    which_ref[...] = jnp.broadcast_to(own_column(assign_ref, tall, request_rows, core_count), which_ref.shape)
    live_ref[...] = jnp.broadcast_to(own_column(lengths_ref, tall, request_rows, core_count), live_ref.shape)
    for copy in copies:
        copy.wait()


def attend_kernel(
    q_ref, stored_values, keys_ref, skeys_ref, svalues_ref, which_ref, live_ref, ride_ref, out_ref, values_ref, sem
):
    fetch = pltpu.make_async_copy(stored_values, values_ref, sem)
    fetch.start()
    seq_count, span, group_width = q_ref.shape
    requests = seq_count * span
    per_kv = NQH // KVH
    width = keys_ref.shape[2]
    heads_here = width // HD
    length = keys_ref.shape[1] // NPFX
    slots = skeys_ref.shape[3]
    queries = q_ref[...].reshape(requests, group_width)
    heads = [(h, j) for h in range(heads_here) for j in range(per_kv)]
    query = {(h, j): queries[:, (h * per_kv + j) * HD : (h * per_kv + j + 1) * HD] for h, j in heads}
    query32 = {key: value.astype(jnp.float32) for key, value in query.items()}
    blank = jnp.zeros((span, HD), jnp.float32)
    tall = span * len(heads)
    column = lax.broadcasted_iota(jnp.int32, (tall, span * slots), 1)
    low = lax.broadcasted_iota(jnp.int32, (tall, span * slots), 0) % span * slots
    added, more, found = {}, {}, []
    blocks = [slice(b * span, (b + 1) * span) for b in range(seq_count)]
    for rows in blocks:
        part = jnp.concatenate(
            [
                jnp.concatenate([query32[h, j][rows] if g == h else blank for g in range(heads_here)], axis=1)
                for h, j in heads
            ],
            axis=0,
        ).astype(jnp.bfloat16)
        skeys = skeys_ref[0, 0, rows].reshape(span * slots, width)
        found.append(lax.dot_general(part, skeys, NT, preferred_element_type=jnp.float32))
    for b, rows in enumerate(blocks):
        live = jnp.concatenate([live_ref[rows, :1]] * len(heads), axis=0)
        found[b] = jnp.where((column >= low) & (column < low + live), weigh(found[b]), 0.0)
    for b, rows in enumerate(blocks):
        svalues = svalues_ref[0, 0, rows].reshape(span * slots, width)
        sums = jnp.sum(found[b], axis=1, keepdims=True)
        products = jnp.dot(found[b].astype(jnp.bfloat16), svalues, preferred_element_type=jnp.float32)
        for i, (h, j) in enumerate(heads):
            more[h, j, b] = sums[i * span : (i + 1) * span]
            added[h, j, b] = products[i * span : (i + 1) * span, h * HD : (h + 1) * HD]
    results = []
    fetch.wait()
    for h in range(heads_here):
        columns = slice(h * HD, (h + 1) * HD)
        stacked = jnp.concatenate([query[h, j] for j in range(per_kv)], axis=0)
        scores = lax.dot_general(stacked, keys_ref[0, :length, columns], NT, preferred_element_type=jnp.float32)
        for p in range(1, NPFX):
            other = lax.dot_general(
                stacked, keys_ref[0, p * length : (p + 1) * length, columns], NT, preferred_element_type=jnp.float32
            )
            scores = jnp.where(which_ref[:, :1] == p, other, scores)
        weights = weigh(scores)
        total = jnp.sum(weights, axis=1, keepdims=True)
        rounded = weights.astype(jnp.bfloat16)
        numerator = jnp.dot(rounded, values_ref[0, :length, columns], preferred_element_type=jnp.float32)
        for p in range(1, NPFX):
            other = jnp.dot(
                rounded, values_ref[0, p * length : (p + 1) * length, columns], preferred_element_type=jnp.float32
            )
            numerator = jnp.where(which_ref[...] == p, other, numerator)

        def regroup(parts):
            return jnp.concatenate([parts[h, j, b] for j in range(per_kv) for b in range(seq_count)], axis=0)

        result = (numerator + regroup(added)) * (1.0 / (total + regroup(more)))
        for j in range(per_kv):
            results.append(result[j * requests : (j + 1) * requests].reshape(seq_count, span, HD))
    for c in range(heads_here):
        out_ref[:, : per_kv * span, c * HD : (c + 1) * HD] = jnp.concatenate(
            [results[t * heads_here + c] for t in range(per_kv)], axis=1
        ).astype(jnp.bfloat16)
    out_ref[:, per_kv * span :, :] = ride_ref[...]


def forward_kernel(*refs):
    *pieces, out_ref = refs
    for j, piece in enumerate(pieces):
        out_ref[j] = piece[1]


def forward(pieces):
    return pl.pallas_call(
        forward_kernel,
        out_shape=jax.ShapeDtypeStruct((len(pieces), *pieces[0].shape[1:]), pieces[0].dtype),
        in_specs=[VMEM] * len(pieces),
        out_specs=VMEM,
        cost_estimate=pl.CostEstimate(flops=2**34, bytes_accessed=1000, transcendentals=0),
    )(*(pin(piece) for piece in pieces))


def finish_kernel(count, back_ref, far_ref, *refs):
    *near, cache_ref, attention_ref, sems = refs
    place = lax.axis_index("seq")
    rows = cache_ref.shape[3]
    request_rows = attention_ref.shape[0]
    width = back_ref.shape[2]
    parts = attention_ref.shape[1] // (count * width)
    riding = back_ref.shape[1] - parts * request_rows
    copies = []
    for j in range(count // 2):
        for d, piece in ((0, near[j].at[0]), (1, far_ref.at[j])):
            source = jnp.bitwise_xor(place, 2 * j + d)
            copies += [
                pltpu.make_async_copy(piece.at[:rows], cache_ref.at[0, 0, source], sems.at[2 * j + d, 0]),
                pltpu.make_async_copy(
                    piece.at[rows:], cache_ref.at[1, 0, source, : rows - riding], sems.at[2 * j + d, 1]
                ),
            ]
    copies.append(
        pltpu.make_async_copy(
            back_ref.at[:, parts * request_rows :], cache_ref.at[1, 0, :, rows - riding :], sems.at[0, 2]
        )
    )
    for copy in copies:
        copy.start()
    for s in range(count):
        block = back_ref[s, : parts * request_rows].astype(jnp.float32)
        for t in range(parts):
            attention_ref[:, (s * parts + t) * width : (s * parts + t + 1) * width] = block[
                t * request_rows : (t + 1) * request_rows
            ].astype(jnp.bfloat16)
    for copy in copies:
        copy.wait()


def local(new_kv, old_keys, old_values, suffix_keys, suffix_values, queries, lengths, assign):
    seq_count = lax.axis_size("seq")
    core_count = lax.axis_size("pd")
    if seq_count > KVH or seq_count & (seq_count - 1):
        return general(new_kv, old_keys, old_values, suffix_keys, suffix_values, queries, lengths, assign)
    half = seq_count // 2
    request_rows = queries.shape[0]
    prefix_rows = new_kv.shape[1]
    group_width = queries.shape[1] // seq_count
    width = new_kv.shape[2] // seq_count
    tall = NQH // KVH * seq_count * request_rows
    prefix_length = prefix_rows * seq_count * core_count // NPFX
    rates = (10000.0 ** (-2.0 * (np.arange(HD) % (HD // 2)) / HD)).astype(np.float32)

    def swap(x, k):
        return lax.ppermute(x, "seq", [(i, i ^ k) for i in range(seq_count)])

    asked = lax.all_to_all(
        queries.reshape(request_rows, seq_count, group_width).transpose(1, 0, 2), "seq", 0, 0, tiled=True
    )
    stored = (old_keys, suffix_keys, suffix_values)
    riding = 32
    piece = (2, 2 * prefix_rows - riding, width)
    packed = NQH // KVH * request_rows + riding
    column = pltpu.VMEM((tall, WIDE), jnp.int32)
    prepared = pl.pallas_call(
        functools.partial(prepare_kernel, seq_count, core_count, prefix_length, request_rows, riding),
        out_shape=[pltpu.VMEM(piece, jnp.bfloat16)]
        + [pltpu.HBM(piece, jnp.bfloat16)] * (half - 1)
        + [column] * 2
        + [pltpu.VMEM((seq_count, riding, width), jnp.bfloat16)]
        + [pltpu.VMEM(x.shape, x.dtype) for x in stored],
        in_specs=[HBM] * 7,
        out_specs=[VMEM] + [HBM] * (half - 1) + [VMEM] * 6,
        scratch_shapes=[
            pltpu.VMEM((1, HD), jnp.float32),
            pltpu.VMEM((1, assign.shape[0]), jnp.int32),
            pltpu.VMEM((1, assign.shape[0]), jnp.int32),
            pltpu.VMEM(new_kv.shape, jnp.bfloat16),
            pltpu.VMEM((half - 1, *piece), jnp.bfloat16),
            pltpu.SemaphoreType.DMA((7,)),
            pltpu.SemaphoreType.DMA((half - 1,)),
        ],
        cost_estimate=pl.CostEstimate(flops=2**33, bytes_accessed=1000, transcendentals=0),
        compiler_params=pltpu.CompilerParams(vmem_limit_bytes=16 * 2**20),
    )(
        *(
            pin(x, pltpu.HBM)
            for x in (
                jnp.asarray(rates).reshape(1, HD), assign.reshape(1, -1), lengths.reshape(1, -1), new_kv, *stored
            )
        )
    )
    kv_cuts, (which, live, ride, *fetched) = prepared[:half], prepared[half:]
    kv_near = [kv_cuts[0]]
    for j in range(1, half):
        kv_near.append(swap(kv_cuts[j], 2 * j))
    attended = pl.pallas_call(
        attend_kernel,
        out_shape=pltpu.VMEM((seq_count, packed, width), jnp.bfloat16),
        in_specs=[VMEM, HBM] + [VMEM] * 6,
        out_specs=VMEM,
        scratch_shapes=[pltpu.VMEM(old_values.shape, jnp.bfloat16), pltpu.SemaphoreType.DMA(())],
        compiler_params=pltpu.CompilerParams(vmem_limit_bytes=16 * 2**20),
        cost_estimate=pl.CostEstimate(flops=2**30, bytes_accessed=2**20, transcendentals=2**10),
    )(pin(asked), pin(old_values, pltpu.HBM), *(pin(x) for x in fetched), pin(which), pin(live), pin(ride))
    kv_far = swap(forward(kv_near), 1)
    back = lax.all_to_all(attended, "seq", 0, 0, tiled=True)
    return tuple(
        pl.pallas_call(
            functools.partial(finish_kernel, seq_count),
            out_shape=(
                jax.ShapeDtypeStruct((2, 1, seq_count, prefix_rows, width), jnp.bfloat16),
                jax.ShapeDtypeStruct((request_rows, NQH * HD), jnp.bfloat16),
            ),
            in_specs=[VMEM] * (half + 2),
            out_specs=(HBM, VMEM),
            scratch_shapes=[pltpu.SemaphoreType.DMA((seq_count, 3))],
            cost_estimate=pl.CostEstimate(flops=0, bytes_accessed=2**20, transcendentals=0),
        )(*(pin(x) for x in (back, kv_far, *kv_near)))
    )


def solution(mesh):
    return jax.shard_map(
        local,
        mesh=mesh,
        in_specs=(
            P("grp", ("seq", "pd"), None),
            P("seq", "grp", None),
            P("seq", "grp", None),
            P("pd", "seq", "grp", None, None),
            P("pd", "seq", "grp", None, None),
            P(("seq", "pd"), "grp"),
            P("grp"),
            P("grp"),
        ),
        out_specs=(P(None, "seq", "grp", "pd", None), P(("seq", "pd"), "grp")),
        check_vma=False,
    )
```

```python
import functools
import math

import jax
import jax.numpy as jnp
import numpy as np
from jax import lax
from jax.experimental import pallas as pl
from jax.experimental.pallas import tpu as pltpu
from jax.sharding import PartitionSpec as P

HD = 128
KVH = 16
NQH = 32
NPFX = 2


softcap = 50.0
query_scale = 1.0 / 12.0


def rotary(key_rows, positions):
    head_width = key_rows.shape[-1]
    halfway = head_width // 2
    inverse = 10000.0 ** (-2.0 * jnp.arange(halfway).astype(jnp.float32) / head_width)
    angles = positions.astype(jnp.float32)[:, None] * inverse[None, :]
    angles = jnp.concatenate([angles, angles], axis=1)
    values = key_rows.astype(jnp.float32)
    turned = jnp.concatenate([-values[..., halfway:], values[..., :halfway]], axis=-1)
    return values * jnp.cos(angles)[:, None, :] + turned * jnp.sin(angles)[:, None, :]


def capped(scores):
    return softcap * jnp.tanh(scores * query_scale / softcap)


def general(new_kv, old_keys, old_values, suffix_keys, suffix_values, queries, lengths, assign):
    seq_count = lax.axis_size("seq")
    core_count = lax.axis_size("pd")
    seq_place = lax.axis_index("seq")
    core_place = lax.axis_index("pd")
    per_kv = NQH // KVH
    sub_blocks = max(seq_count // KVH, 1)
    heads_here = max(KVH // seq_count, 1)
    head_groups = KVH // heads_here
    prefix_rows = new_kv.shape[1]
    request_rows = queries.shape[0]
    prefix_length = prefix_rows * seq_count * core_count // NPFX
    group_width = heads_here * per_kv * HD
    positions = (
        (seq_place * core_count + core_place) * prefix_rows
        + jnp.arange(prefix_rows, dtype=jnp.int32)
    ) % prefix_length
    rotated = rotary(new_kv[0].reshape(prefix_rows, KVH, HD), positions).astype(jnp.bfloat16)
    rotated = rotated.reshape(prefix_rows, KVH * HD)
    outgoing = jnp.stack([rotated, new_kv[1]]).reshape(
        2, prefix_rows // sub_blocks, seq_count, heads_here * HD
    )
    arrived = lax.all_to_all(outgoing, "seq", split_axis=2, concat_axis=1, tiled=True)
    new_cache = arrived.reshape(2, 1, seq_count, prefix_rows // sub_blocks, heads_here * HD)
    head_group = seq_place % head_groups
    token_block = seq_place // head_groups
    half_rows = seq_count * request_rows
    gathered = lax.all_gather(queries, "seq", axis=0, tiled=True)
    own_queries = lax.dynamic_slice_in_dim(gathered, head_group * group_width, group_width, 1)
    query_blocks = own_queries.reshape(half_rows, heads_here, per_kv, HD)
    own_assign = lax.dynamic_index_in_dim(
        assign.reshape(seq_count, core_count, request_rows), core_place, 1, keepdims=False
    ).reshape(half_rows)
    own_lengths = lax.dynamic_index_in_dim(
        lengths.reshape(seq_count, core_count, request_rows), core_place, 1, keepdims=False
    ).reshape(half_rows)
    prefix_keys = old_keys[0].reshape(-1, heads_here, HD)
    prefix_values = old_values[0].reshape(-1, heads_here, HD)
    token_count = prefix_keys.shape[0]
    token_prefix = (
        jnp.arange(token_count, dtype=jnp.int32) * sub_blocks + token_block
    ) // prefix_length
    block_rows = math.gcd(half_rows, 256)

    def prefix_block(block_index):
        row_start = block_index * block_rows
        query_part = lax.dynamic_slice_in_dim(query_blocks, row_start, block_rows, 0)
        assign_part = lax.dynamic_slice_in_dim(own_assign, row_start, block_rows, 0)
        scores = capped(
            jnp.einsum(
                "rhqd,thd->rhqt", query_part, prefix_keys, preferred_element_type=jnp.float32
            )
        )
        allowed = (assign_part[:, None] == token_prefix[None, :])[:, None, None, :]
        weights = jnp.where(allowed, jnp.exp(scores), 0.0)
        totals = jnp.sum(weights, axis=-1)
        numerators = jnp.einsum(
            "rhqt,thd->rhqd",
            weights.astype(jnp.bfloat16),
            prefix_values,
            preferred_element_type=jnp.float32,
        )
        return (totals, numerators)

    totals, numerators = lax.map(prefix_block, jnp.arange(half_rows // block_rows, dtype=jnp.int32))
    totals = totals.reshape(half_rows, heads_here, per_kv)
    numerators = numerators.reshape(half_rows, heads_here, per_kv, HD)
    suffix_rows = head_groups * request_rows
    suffix_start = token_block * suffix_rows
    suffix_query = lax.dynamic_slice_in_dim(query_blocks, suffix_start, suffix_rows, 0)
    suffix_length = lax.dynamic_slice_in_dim(own_lengths, suffix_start, suffix_rows, 0)
    recent_keys = suffix_keys[0, 0].reshape(suffix_rows, -1, heads_here, HD)
    recent_values = suffix_values[0, 0].reshape(suffix_rows, -1, heads_here, HD)
    recent_scores = capped(
        jnp.einsum("rhqd,rphd->rhqp", suffix_query, recent_keys, preferred_element_type=jnp.float32)
    )
    live_slots = jnp.arange(recent_keys.shape[1], dtype=jnp.int32)[None, :] < suffix_length[:, None]
    recent_weights = jnp.where(live_slots[:, None, None, :], jnp.exp(recent_scores), 0.0)
    recent_totals = jnp.sum(recent_weights, axis=-1)
    recent_numerators = jnp.einsum(
        "rhqp,rphd->rhqd",
        recent_weights.astype(jnp.bfloat16),
        recent_values,
        preferred_element_type=jnp.float32,
    )
    totals = lax.dynamic_update_slice_in_dim(
        totals,
        lax.dynamic_slice_in_dim(totals, suffix_start, suffix_rows, 0) + recent_totals,
        suffix_start,
        0,
    )
    numerators = lax.dynamic_update_slice_in_dim(
        numerators,
        lax.dynamic_slice_in_dim(numerators, suffix_start, suffix_rows, 0) + recent_numerators,
        suffix_start,
        0,
    )
    back_numerators, back_totals = (
        lax.all_to_all(
            numerators.reshape(seq_count, request_rows, group_width),
            "seq",
            split_axis=0,
            concat_axis=0,
            tiled=True,
        ),
        lax.all_to_all(
            totals.reshape(seq_count, request_rows, heads_here * per_kv),
            "seq",
            split_axis=0,
            concat_axis=0,
            tiled=True,
        ),
    )
    back_numerators = back_numerators.reshape(
        sub_blocks, head_groups, request_rows, heads_here * per_kv, HD
    ).sum(0)
    back_totals = back_totals.reshape(
        sub_blocks, head_groups, request_rows, heads_here * per_kv
    ).sum(0)
    attention = (
        (back_numerators / back_totals[..., None])
        .transpose(1, 0, 2, 3)
        .reshape(request_rows, NQH * HD)
    )
    return (new_cache, attention.astype(jnp.bfloat16))


def weigh(scores):
    return jnp.exp2((softcap * math.log2(math.e)) * jnp.tanh(scores * (query_scale / softcap)))


NT = (((1,), (1,)), ((), ()))
NN = (((1,), (0,)), ((), ()))


def pin(x, space=pltpu.VMEM):
    return pltpu.with_memory_space_constraint(x, space)


VMEM = pl.BlockSpec(memory_space=pltpu.VMEM)
HBM = pl.BlockSpec(memory_space=pltpu.HBM)


def own_column(values_ref, tall, request_rows, core_count):
    shape = (tall, values_ref.shape[1])
    row = lax.broadcasted_iota(jnp.int32, shape, 0) % (values_ref.shape[1] // core_count)
    wanted = (row // request_rows * core_count + lax.axis_index("pd")) * request_rows + row % request_rows
    picked = jnp.where(lax.broadcasted_iota(jnp.int32, shape, 1) == wanted, values_ref[...], 0)
    return jnp.sum(picked.astype(jnp.float32), axis=1, keepdims=True).astype(jnp.int32)


def prepare_kernel(count, core_count, prefix_length, riding, *refs):
    (stored_rates, stored_kv), stored, refs = refs[:2], refs[2:5], refs[5:]
    own_ref, *pieces = refs[: count // 2]
    ride_ref, *fetched = refs[count // 2 : count // 2 + 4]
    rates_ref, kv_ref, sems = refs[count // 2 + 4 :]
    first_copies = [
        pltpu.make_async_copy(a, b, sems.at[i])
        for i, (a, b) in enumerate(
            (
                (stored_rates, rates_ref),
                (stored_kv, kv_ref),
            )
        )
    ]
    copies = [pltpu.make_async_copy(a, b, sems.at[2 + i]) for i, (a, b) in enumerate(zip(stored, fetched))]
    for copy in first_copies + copies:
        copy.start()
    first_copies[0].wait()
    place = lax.axis_index("seq")
    rows = kv_ref.shape[1]
    width = kv_ref.shape[2] // count
    first = (place * core_count + lax.axis_index("pd")) * rows
    position = (first + lax.broadcasted_iota(jnp.int32, (rows, HD), 0)) % prefix_length
    angles = position.astype(jnp.float32) * rates_ref[...]
    cosine = jnp.cos(angles)
    sine = jnp.sin(angles)
    sine = jnp.where(lax.broadcasted_iota(jnp.int32, (rows, HD), 1) < HD // 2, -sine, sine)
    for copy in first_copies[1:]:
        copy.wait()
    for j in reversed(range(count // 2)):
        cut = pieces[j - 1] if j else own_ref
        for d in range(2):
            start = jnp.bitwise_xor(place, 2 * j + d) * width
            for h in range(width // HD):
                columns = pl.ds(pl.multiple_of(start + h * HD, HD), HD)
                keys = kv_ref[0, :, columns].astype(jnp.float32)
                turned = pltpu.roll(keys, HD // 2, 1)
                cut[d, :rows, h * HD : (h + 1) * HD] = (keys * cosine + turned * sine).astype(jnp.bfloat16)
                cut[d, rows:, h * HD : (h + 1) * HD] = kv_ref[1, : rows - riding, columns]
    for s in range(count):
        ride_ref[s] = kv_ref[1, rows - riding :, s * width : (s + 1) * width]
    for copy in copies:
        copy.wait()


def fetch(stored, target, sems):
    parts = sems.shape[0]
    leading = stored.shape[:-3] if len(stored.shape) > 3 else stored.shape[:1]
    index = (0,) * len(leading)
    rows = stored.shape[len(leading)] // parts
    copies = []
    for i in range(parts):
        at = (*index, pl.ds(i * rows, rows))
        copies.append(pltpu.make_async_copy(stored.at[at], target.at[at], sems.at[i]))
        copies[-1].start()
    return copies


def attend_kernel(
    core_count, q_ref, stored_assign, stored_lengths, stored_svalues,
    keys_ref, skeys_ref, values_ref, ride_ref, stored_out, svalues_ref, out_ref, assign_ref, lengths_ref, sems, out_sems,
):
    small = [
        pltpu.make_async_copy(stored_assign, assign_ref, out_sems.at[2]),
        pltpu.make_async_copy(stored_lengths, lengths_ref, out_sems.at[3]),
    ]
    for copy in small:
        copy.start()
    fetches = [
        fetch(a, b, sems.at[i]) for i, (a, b) in enumerate(((stored_svalues, svalues_ref),))
    ]
    seq_count, span, group_width = q_ref.shape
    requests = seq_count * span
    per_kv = NQH // KVH
    width = keys_ref.shape[2]
    heads_here = width // HD
    length = keys_ref.shape[1] // NPFX
    slots = skeys_ref.shape[3]
    queries = q_ref[...].reshape(requests, group_width)
    heads = [(h, j) for h in range(heads_here) for j in range(per_kv)]
    query = {(h, j): queries[:, (h * per_kv + j) * HD : (h * per_kv + j + 1) * HD] for h, j in heads}
    query32 = {key: value.astype(jnp.float32) for key, value in query.items()}
    blank = jnp.zeros((span, HD), jnp.float32)
    tall = span * len(heads)
    column = lax.broadcasted_iota(jnp.int32, (tall, span * slots), 1)
    low = lax.broadcasted_iota(jnp.int32, (tall, span * slots), 0) % span * slots
    ride = pltpu.make_async_copy(ride_ref, stored_out.at[:, per_kv * span :], out_sems.at[0])
    ride.start()
    for copy in small:
        copy.wait()
    which = own_column(assign_ref, per_kv * requests, span, core_count)
    live = own_column(lengths_ref, requests, span, core_count)
    scores = []
    for h in range(heads_here):
        columns = slice(h * HD, (h + 1) * HD)
        stacked = jnp.concatenate([query[h, j] for j in range(per_kv)], axis=0)
        chosen = lax.dot_general(stacked, keys_ref[0, :length, columns], NT, preferred_element_type=jnp.float32)
        for p in range(1, NPFX):
            other = lax.dot_general(
                stacked, keys_ref[0, p * length : (p + 1) * length, columns], NT, preferred_element_type=jnp.float32
            )
            chosen = jnp.where(which == p, other, chosen)
        scores.append(chosen)
    blocks = [slice(b * span, (b + 1) * span) for b in range(seq_count)]
    parts = [
        jnp.concatenate(
            [
                jnp.concatenate([query32[h, j][rows] if g == h else blank for g in range(heads_here)], axis=1)
                for h, j in heads
            ],
            axis=0,
        ).astype(jnp.bfloat16)
        for rows in blocks
    ]
    found = [
        lax.dot_general(
            part, skeys_ref[0, 0, rows].reshape(span * slots, width), NT, preferred_element_type=jnp.float32
        )
        for rows, part in zip(blocks, parts)
    ]
    weights = [weigh(chosen) for chosen in scores]
    for b, rows in enumerate(blocks):
        slots_live = jnp.concatenate([live[rows]] * len(heads), axis=0)
        found[b] = jnp.where((column >= low) & (column < low + slots_live), weigh(found[b]), 0.0)
    numerators = []
    for h in range(heads_here):
        columns = slice(h * HD, (h + 1) * HD)
        rounded = weights[h].astype(jnp.bfloat16)
        numerator = jnp.dot(rounded, values_ref[0, :length, columns], preferred_element_type=jnp.float32)
        for p in range(1, NPFX):
            other = jnp.dot(
                rounded, values_ref[0, p * length : (p + 1) * length, columns], preferred_element_type=jnp.float32
            )
            numerator = jnp.where(which == p, other, numerator)
        numerators.append(numerator)
    added, more = {}, {}
    for copy in fetches[0]:
        copy.wait()
    for b, rows in enumerate(blocks):
        svalues = svalues_ref[0, 0, rows].reshape(span * slots, width)
        sums = jnp.sum(found[b], axis=1, keepdims=True)
        products = jnp.dot(found[b].astype(jnp.bfloat16), svalues, preferred_element_type=jnp.float32)
        for i, (h, j) in enumerate(heads):
            more[h, j, b] = sums[i * span : (i + 1) * span]
            added[h, j, b] = products[i * span : (i + 1) * span, h * HD : (h + 1) * HD]
    results = []
    for h in range(heads_here):

        def regroup(cut):
            return jnp.concatenate([cut[h, j, b] for j in range(per_kv) for b in range(seq_count)], axis=0)

        total = jnp.sum(weights[h], axis=1, keepdims=True) + regroup(more)
        result = (numerators[h] + regroup(added)) * (1.0 / total)
        for j in range(per_kv):
            results.append(result[j * requests : (j + 1) * requests].reshape(seq_count, span, HD))
    for c in range(heads_here):
        out_ref[:, :, c * HD : (c + 1) * HD] = jnp.concatenate(
            [results[t * heads_here + c] for t in range(per_kv)], axis=1
        ).astype(jnp.bfloat16)
    out = pltpu.make_async_copy(out_ref, stored_out.at[:, : per_kv * span], out_sems.at[1])
    out.start()
    ride.wait()
    out.wait()


def forward_kernel(*refs):
    *pieces, out_ref = refs
    for j, piece in enumerate(pieces):
        out_ref[j] = piece[1]


def forward(pieces):
    return pl.pallas_call(
        forward_kernel,
        out_shape=pltpu.VMEM((len(pieces), *pieces[0].shape[1:]), pieces[0].dtype),
        in_specs=[VMEM] * len(pieces),
        out_specs=VMEM,
        cost_estimate=pl.CostEstimate(flops=2**34, bytes_accessed=1000, transcendentals=0),
    )(*(pin(piece) for piece in pieces))


def finish_kernel(count, back_ref, far_ref, *refs):
    *near, cache_ref, stored_attention, attention_ref, sems = refs
    place = lax.axis_index("seq")
    rows = cache_ref.shape[3]
    request_rows = attention_ref.shape[0]
    width = back_ref.shape[2]
    parts = attention_ref.shape[1] // (count * width)
    riding = back_ref.shape[1] - parts * request_rows
    copies = []
    for j in range(count // 2):
        for d, piece in ((0, near[j].at[0]), (1, far_ref.at[j])):
            source = jnp.bitwise_xor(place, 2 * j + d)
            copies += [
                pltpu.make_async_copy(piece.at[:rows], cache_ref.at[0, 0, source], sems.at[2 * j + d, 0]),
                pltpu.make_async_copy(
                    piece.at[rows:], cache_ref.at[1, 0, source, : rows - riding], sems.at[2 * j + d, 1]
                ),
            ]
    copies.append(
        pltpu.make_async_copy(
            back_ref.at[:, parts * request_rows :], cache_ref.at[1, 0, :, rows - riding :], sems.at[0, 2]
        )
    )
    for copy in copies:
        copy.start()
    copies.append(pltpu.make_async_copy(attention_ref, stored_attention, sems.at[1, 2]))
    for s in range(count):
        block = back_ref[s, : parts * request_rows].astype(jnp.float32)
        for t in range(parts):
            attention_ref[:, (s * parts + t) * width : (s * parts + t + 1) * width] = block[
                t * request_rows : (t + 1) * request_rows
            ].astype(jnp.bfloat16)
    copies[-1].start()
    for copy in copies:
        copy.wait()


def local(new_kv, old_keys, old_values, suffix_keys, suffix_values, queries, lengths, assign):
    seq_count = lax.axis_size("seq")
    core_count = lax.axis_size("pd")
    if seq_count > KVH or seq_count & (seq_count - 1):
        return general(new_kv, old_keys, old_values, suffix_keys, suffix_values, queries, lengths, assign)
    half = seq_count // 2
    request_rows = queries.shape[0]
    prefix_rows = new_kv.shape[1]
    group_width = queries.shape[1] // seq_count
    width = new_kv.shape[2] // seq_count
    prefix_length = prefix_rows * seq_count * core_count // NPFX
    rates = (10000.0 ** (-2.0 * (np.arange(HD) % (HD // 2)) / HD)).astype(np.float32)

    def swap(x, k):
        return lax.ppermute(x, "seq", [(i, i ^ k) for i in range(seq_count)])

    asked = lax.all_to_all(
        queries.reshape(request_rows, seq_count, group_width).transpose(1, 0, 2), "seq", 0, 0, tiled=True
    )
    early = (old_keys, suffix_keys, old_values, )
    late = (suffix_values,)
    riding = 32
    piece = (2, 2 * prefix_rows - riding, width)
    packed = NQH // KVH * request_rows + riding
    prepared = pl.pallas_call(
        functools.partial(prepare_kernel, seq_count, core_count, prefix_length, riding),
        out_shape=[pltpu.VMEM(piece, jnp.bfloat16)]
        + [pltpu.VMEM(piece, jnp.bfloat16)] * (half - 1)
        + [pltpu.VMEM((seq_count, riding, width), jnp.bfloat16)]
        + [pltpu.VMEM(x.shape, x.dtype) for x in early],
        in_specs=[HBM] * 5,
        out_specs=[VMEM] * (half + 4),
        scratch_shapes=[
            pltpu.VMEM((1, HD), jnp.float32),
            pltpu.VMEM(new_kv.shape, jnp.bfloat16),
            pltpu.SemaphoreType.DMA((5,)),
        ],
        cost_estimate=pl.CostEstimate(flops=2**33, bytes_accessed=1000, transcendentals=0),
        compiler_params=pltpu.CompilerParams(vmem_limit_bytes=16 * 2**20),
    )(
        *(
            pin(x, pltpu.HBM)
            for x in (
                jnp.asarray(rates).reshape(1, HD), new_kv, *early
            )
        )
    )
    kv_cuts, (ride, *fetched) = prepared[:half], prepared[half:]
    kv_near = [kv_cuts[0]]
    for j in range(1, half):
        kv_near.append(swap(kv_cuts[j], 2 * j))
    attended = pl.pallas_call(
        functools.partial(attend_kernel, core_count),
        out_shape=pltpu.HBM((seq_count, packed, width), jnp.bfloat16),
        in_specs=[VMEM] + [HBM] * (2 + len(late)) + [VMEM] * (len(early) + 1),
        out_specs=HBM,
        scratch_shapes=[
            *(pltpu.VMEM(x.shape, x.dtype) for x in late),
            pltpu.VMEM((seq_count, packed - riding, width), jnp.bfloat16),
            pltpu.VMEM((1, assign.shape[0]), jnp.int32),
            pltpu.VMEM((1, assign.shape[0]), jnp.int32),
            pltpu.SemaphoreType.DMA((len(late), 4)),
            pltpu.SemaphoreType.DMA((4,)),
        ],
        compiler_params=pltpu.CompilerParams(vmem_limit_bytes=16 * 2**20),
        cost_estimate=pl.CostEstimate(flops=2**30, bytes_accessed=2**20, transcendentals=2**10),
    )(
        pin(asked),
        *(pin(x, pltpu.HBM) for x in (assign.reshape(1, -1), lengths.reshape(1, -1), *late)),
        *(pin(x) for x in fetched),
        pin(ride),
    )
    kv_far = swap(forward(kv_near), 1)
    back = lax.all_to_all(attended, "seq", 0, 0, tiled=True)
    return tuple(
        pl.pallas_call(
            functools.partial(finish_kernel, seq_count),
            out_shape=(
                jax.ShapeDtypeStruct((2, 1, seq_count, prefix_rows, width), jnp.bfloat16),
                jax.ShapeDtypeStruct((request_rows, NQH * HD), jnp.bfloat16),
            ),
            in_specs=[VMEM] * (half + 2),
            out_specs=(HBM, HBM),
            scratch_shapes=[
                pltpu.VMEM((request_rows, NQH * HD), jnp.bfloat16),
                pltpu.SemaphoreType.DMA((seq_count, 3)),
            ],
            cost_estimate=pl.CostEstimate(flops=0, bytes_accessed=2**20, transcendentals=0),
        )(*(pin(x) for x in (back, kv_far, *kv_near)))
    )


def solution(mesh):
    return jax.shard_map(
        local,
        mesh=mesh,
        in_specs=(
            P("grp", ("seq", "pd"), None),
            P("seq", "grp", None),
            P("seq", "grp", None),
            P("pd", "seq", "grp", None, None),
            P("pd", "seq", "grp", None, None),
            P(("seq", "pd"), "grp"),
            P("grp"),
            P("grp"),
        ),
        out_specs=(P(None, "seq", "grp", "pd", None), P(("seq", "pd"), "grp")),
        check_vma=False,
    )
```

```python
import functools
import math

import jax
import jax.numpy as jnp
from jax import lax
from jax.experimental import pallas as pl
from jax.experimental.pallas import tpu as pltpu
from jax.sharding import PartitionSpec as P

HD = 128
KVH = 16
NQH = 32
NPFX = 2


softcap = 50.0
query_scale = 1.0 / 12.0


def rotary(key_rows, positions):
    head_width = key_rows.shape[-1]
    halfway = head_width // 2
    inverse = 10000.0 ** (-2.0 * jnp.arange(halfway).astype(jnp.float32) / head_width)
    angles = positions.astype(jnp.float32)[:, None] * inverse[None, :]
    angles = jnp.concatenate([angles, angles], axis=1)
    values = key_rows.astype(jnp.float32)
    turned = jnp.concatenate([-values[..., halfway:], values[..., :halfway]], axis=-1)
    return values * jnp.cos(angles)[:, None, :] + turned * jnp.sin(angles)[:, None, :]


def capped(scores):
    return softcap * jnp.tanh(scores * query_scale / softcap)


def general(new_kv, old_keys, old_values, suffix_keys, suffix_values, queries, lengths, assign):
    seq_count = lax.axis_size("seq")
    core_count = lax.axis_size("pd")
    seq_place = lax.axis_index("seq")
    core_place = lax.axis_index("pd")
    per_kv = NQH // KVH
    sub_blocks = max(seq_count // KVH, 1)
    heads_here = max(KVH // seq_count, 1)
    head_groups = KVH // heads_here
    prefix_rows = new_kv.shape[1]
    request_rows = queries.shape[0]
    prefix_length = prefix_rows * seq_count * core_count // NPFX
    group_width = heads_here * per_kv * HD
    positions = (
        (seq_place * core_count + core_place) * prefix_rows
        + jnp.arange(prefix_rows, dtype=jnp.int32)
    ) % prefix_length
    rotated = rotary(new_kv[0].reshape(prefix_rows, KVH, HD), positions).astype(jnp.bfloat16)
    rotated = rotated.reshape(prefix_rows, KVH * HD)
    outgoing = jnp.stack([rotated, new_kv[1]]).reshape(
        2, prefix_rows // sub_blocks, seq_count, heads_here * HD
    )
    arrived = lax.all_to_all(outgoing, "seq", split_axis=2, concat_axis=1, tiled=True)
    new_cache = arrived.reshape(2, 1, seq_count, prefix_rows // sub_blocks, heads_here * HD)
    head_group = seq_place % head_groups
    token_block = seq_place // head_groups
    half_rows = seq_count * request_rows
    gathered = lax.all_gather(queries, "seq", axis=0, tiled=True)
    own_queries = lax.dynamic_slice_in_dim(gathered, head_group * group_width, group_width, 1)
    query_blocks = own_queries.reshape(half_rows, heads_here, per_kv, HD)
    own_assign = lax.dynamic_index_in_dim(
        assign.reshape(seq_count, core_count, request_rows), core_place, 1, keepdims=False
    ).reshape(half_rows)
    own_lengths = lax.dynamic_index_in_dim(
        lengths.reshape(seq_count, core_count, request_rows), core_place, 1, keepdims=False
    ).reshape(half_rows)
    prefix_keys = old_keys[0].reshape(-1, heads_here, HD)
    prefix_values = old_values[0].reshape(-1, heads_here, HD)
    token_count = prefix_keys.shape[0]
    token_prefix = (
        jnp.arange(token_count, dtype=jnp.int32) * sub_blocks + token_block
    ) // prefix_length
    block_rows = math.gcd(half_rows, 256)

    def prefix_block(block_index):
        row_start = block_index * block_rows
        query_part = lax.dynamic_slice_in_dim(query_blocks, row_start, block_rows, 0)
        assign_part = lax.dynamic_slice_in_dim(own_assign, row_start, block_rows, 0)
        scores = capped(
            jnp.einsum(
                "rhqd,thd->rhqt", query_part, prefix_keys, preferred_element_type=jnp.float32
            )
        )
        allowed = (assign_part[:, None] == token_prefix[None, :])[:, None, None, :]
        weights = jnp.where(allowed, jnp.exp(scores), 0.0)
        totals = jnp.sum(weights, axis=-1)
        numerators = jnp.einsum(
            "rhqt,thd->rhqd",
            weights.astype(jnp.bfloat16),
            prefix_values,
            preferred_element_type=jnp.float32,
        )
        return (totals, numerators)

    totals, numerators = lax.map(prefix_block, jnp.arange(half_rows // block_rows, dtype=jnp.int32))
    totals = totals.reshape(half_rows, heads_here, per_kv)
    numerators = numerators.reshape(half_rows, heads_here, per_kv, HD)
    suffix_rows = head_groups * request_rows
    suffix_start = token_block * suffix_rows
    suffix_query = lax.dynamic_slice_in_dim(query_blocks, suffix_start, suffix_rows, 0)
    suffix_length = lax.dynamic_slice_in_dim(own_lengths, suffix_start, suffix_rows, 0)
    recent_keys = suffix_keys[0, 0].reshape(suffix_rows, -1, heads_here, HD)
    recent_values = suffix_values[0, 0].reshape(suffix_rows, -1, heads_here, HD)
    recent_scores = capped(
        jnp.einsum("rhqd,rphd->rhqp", suffix_query, recent_keys, preferred_element_type=jnp.float32)
    )
    live_slots = jnp.arange(recent_keys.shape[1], dtype=jnp.int32)[None, :] < suffix_length[:, None]
    recent_weights = jnp.where(live_slots[:, None, None, :], jnp.exp(recent_scores), 0.0)
    recent_totals = jnp.sum(recent_weights, axis=-1)
    recent_numerators = jnp.einsum(
        "rhqp,rphd->rhqd",
        recent_weights.astype(jnp.bfloat16),
        recent_values,
        preferred_element_type=jnp.float32,
    )
    totals = lax.dynamic_update_slice_in_dim(
        totals,
        lax.dynamic_slice_in_dim(totals, suffix_start, suffix_rows, 0) + recent_totals,
        suffix_start,
        0,
    )
    numerators = lax.dynamic_update_slice_in_dim(
        numerators,
        lax.dynamic_slice_in_dim(numerators, suffix_start, suffix_rows, 0) + recent_numerators,
        suffix_start,
        0,
    )
    back_numerators, back_totals = (
        lax.all_to_all(
            numerators.reshape(seq_count, request_rows, group_width),
            "seq",
            split_axis=0,
            concat_axis=0,
            tiled=True,
        ),
        lax.all_to_all(
            totals.reshape(seq_count, request_rows, heads_here * per_kv),
            "seq",
            split_axis=0,
            concat_axis=0,
            tiled=True,
        ),
    )
    back_numerators = back_numerators.reshape(
        sub_blocks, head_groups, request_rows, heads_here * per_kv, HD
    ).sum(0)
    back_totals = back_totals.reshape(
        sub_blocks, head_groups, request_rows, heads_here * per_kv
    ).sum(0)
    attention = (
        (back_numerators / back_totals[..., None])
        .transpose(1, 0, 2, 3)
        .reshape(request_rows, NQH * HD)
    )
    return (new_cache, attention.astype(jnp.bfloat16))


def weigh(scores):
    return jnp.exp2((softcap * math.log2(math.e)) * jnp.tanh(scores * (query_scale / softcap)))


NT = (((1,), (1,)), ((), ()))
NN = (((1,), (0,)), ((), ()))


def pin(x, space=pltpu.VMEM):
    return pltpu.with_memory_space_constraint(x, space)


VMEM = pl.BlockSpec(memory_space=pltpu.VMEM)
HBM = pl.BlockSpec(memory_space=pltpu.HBM)


def own_column(values_ref, tall, request_rows, core_count):
    shape = (tall, values_ref.shape[1])
    row = lax.broadcasted_iota(jnp.int32, shape, 0) % (values_ref.shape[1] // core_count)
    wanted = (row // request_rows * core_count + lax.axis_index("pd")) * request_rows + row % request_rows
    picked = jnp.where(lax.broadcasted_iota(jnp.int32, shape, 1) == wanted, values_ref[...], 0)
    return jnp.sum(picked.astype(jnp.float32), axis=1, keepdims=True).astype(jnp.int32)


def rates_kernel(rates_ref):
    step = lax.broadcasted_iota(jnp.int32, rates_ref.shape, 1) % (HD // 2)
    rates_ref[...] = jnp.exp2(step.astype(jnp.float32) * (-2.0 / HD * math.log2(10000.0)))


def prepare_kernel(count, core_count, prefix_length, riding, rates_ref, kv_ref, *refs):
    *pieces, ride_ref = refs
    place = lax.axis_index("seq")
    rows = kv_ref.shape[1]
    width = kv_ref.shape[2] // count
    first = (place * core_count + lax.axis_index("pd")) * rows
    position = (first + lax.broadcasted_iota(jnp.int32, (rows, HD), 0)) % prefix_length
    angles = position.astype(jnp.float32) * rates_ref[:1]
    cosine = jnp.cos(angles)
    sine = jnp.sin(angles)
    sine = jnp.where(lax.broadcasted_iota(jnp.int32, (rows, HD), 1) < HD // 2, -sine, sine)
    for j in reversed(range(count // 2)):
        for d in range(2):
            start = jnp.bitwise_xor(place, 2 * j + d) * width
            for h in range(width // HD):
                columns = pl.ds(pl.multiple_of(start + h * HD, HD), HD)
                keys = kv_ref[0, :, columns].astype(jnp.float32)
                turned = pltpu.roll(keys, HD // 2, 1)
                pieces[j][d, :rows, h * HD : (h + 1) * HD] = (keys * cosine + turned * sine).astype(jnp.bfloat16)
                pieces[j][d, rows:, h * HD : (h + 1) * HD] = kv_ref[1, : rows - riding, columns]
    for s in range(count):
        ride_ref[s] = kv_ref[1, rows - riding :, s * width : (s + 1) * width]


def fetch(stored, target, sems):
    parts = sems.shape[0]
    leading = stored.shape[:-3] if len(stored.shape) > 3 else stored.shape[:1]
    index = (0,) * len(leading)
    rows = stored.shape[len(leading)] // parts
    copies = []
    for i in range(parts):
        at = (*index, pl.ds(i * rows, rows))
        copies.append(pltpu.make_async_copy(stored.at[at], target.at[at], sems.at[i]))
        copies[-1].start()
    return copies


def attend_kernel(
    core_count, q_ref, stored_assign, stored_lengths, stored_svalues,
    keys_ref, skeys_ref, values_ref, ride_ref, stored_out, svalues_ref, out_ref, assign_ref, lengths_ref, sems, out_sems,
):
    small = [
        pltpu.make_async_copy(stored_assign, assign_ref, out_sems.at[2]),
        pltpu.make_async_copy(stored_lengths, lengths_ref, out_sems.at[3]),
    ]
    for copy in small:
        copy.start()
    fetches = [
        fetch(a, b, sems.at[i]) for i, (a, b) in enumerate(((stored_svalues, svalues_ref),))
    ]
    seq_count, span, group_width = q_ref.shape
    requests = seq_count * span
    per_kv = NQH // KVH
    width = keys_ref.shape[2]
    heads_here = width // HD
    length = keys_ref.shape[1] // NPFX
    slots = skeys_ref.shape[3]
    queries = q_ref[...].reshape(requests, group_width)
    heads = [(h, j) for h in range(heads_here) for j in range(per_kv)]
    query = {(h, j): queries[:, (h * per_kv + j) * HD : (h * per_kv + j + 1) * HD] for h, j in heads}
    query32 = {key: value.astype(jnp.float32) for key, value in query.items()}
    blank = jnp.zeros((span, HD), jnp.float32)
    tall = span * len(heads)
    column = lax.broadcasted_iota(jnp.int32, (tall, span * slots), 1)
    low = lax.broadcasted_iota(jnp.int32, (tall, span * slots), 0) % span * slots
    ride = pltpu.make_async_copy(ride_ref, stored_out.at[:, per_kv * span :], out_sems.at[0])
    ride.start()
    blocks = [slice(b * span, (b + 1) * span) for b in range(seq_count)]
    found = []
    for rows in blocks:
        part = jnp.concatenate(
            [
                jnp.concatenate([query32[h, j][rows] if g == h else blank for g in range(heads_here)], axis=1)
                for h, j in heads
            ],
            axis=0,
        ).astype(jnp.bfloat16)
        skeys = skeys_ref[0, 0, rows].reshape(span * slots, width)
        found.append(lax.dot_general(part, skeys, NT, preferred_element_type=jnp.float32))
    for copy in small:
        copy.wait()
    which = own_column(assign_ref, per_kv * requests, span, core_count)
    live = own_column(lengths_ref, requests, span, core_count)
    added, more = {}, {}
    for b, rows in enumerate(blocks):
        slots_live = jnp.concatenate([live[rows]] * len(heads), axis=0)
        weights = jnp.where((column >= low) & (column < low + slots_live), weigh(found[b]), 0.0)
        sums = jnp.sum(weights, axis=1, keepdims=True)
        for i, (h, j) in enumerate(heads):
            more[h, j, b] = sums[i * span : (i + 1) * span]
        found[b] = weights.astype(jnp.bfloat16)
    numerators, totals = [], []
    for h in range(heads_here):
        columns = slice(h * HD, (h + 1) * HD)
        stacked = jnp.concatenate([query[h, j] for j in range(per_kv)], axis=0)
        scores = lax.dot_general(stacked, keys_ref[0, :length, columns], NT, preferred_element_type=jnp.float32)
        for p in range(1, NPFX):
            other = lax.dot_general(
                stacked, keys_ref[0, p * length : (p + 1) * length, columns], NT, preferred_element_type=jnp.float32
            )
            scores = jnp.where(which == p, other, scores)
        weights = weigh(scores)
        totals.append(jnp.sum(weights, axis=1, keepdims=True))
        rounded = weights.astype(jnp.bfloat16)
        numerator = jnp.dot(rounded, values_ref[0, :length, columns], preferred_element_type=jnp.float32)
        for p in range(1, NPFX):
            other = jnp.dot(
                rounded, values_ref[0, p * length : (p + 1) * length, columns], preferred_element_type=jnp.float32
            )
            numerator = jnp.where(which == p, other, numerator)
        numerators.append(numerator)
    for copy in fetches[0]:
        copy.wait()
    for b, rows in enumerate(blocks):
        svalues = svalues_ref[0, 0, rows].reshape(span * slots, width)
        products = jnp.dot(found[b], svalues, preferred_element_type=jnp.float32)
        for i, (h, j) in enumerate(heads):
            added[h, j, b] = products[i * span : (i + 1) * span, h * HD : (h + 1) * HD]
    results = []
    for h in range(heads_here):

        def regroup(cut):
            return jnp.concatenate([cut[h, j, b] for j in range(per_kv) for b in range(seq_count)], axis=0)

        result = (numerators[h] + regroup(added)) * (1.0 / (totals[h] + regroup(more)))
        for j in range(per_kv):
            results.append(result[j * requests : (j + 1) * requests].reshape(seq_count, span, HD))
    for c in range(heads_here):
        out_ref[:, :, c * HD : (c + 1) * HD] = jnp.concatenate(
            [results[t * heads_here + c] for t in range(per_kv)], axis=1
        ).astype(jnp.bfloat16)
    out = pltpu.make_async_copy(out_ref, stored_out.at[:, : per_kv * span], out_sems.at[1])
    out.start()
    ride.wait()
    out.wait()


def forward_kernel(*refs):
    *pieces, out_ref = refs
    for j, piece in enumerate(pieces):
        out_ref[j] = piece[1]


def forward(pieces):
    return pl.pallas_call(
        forward_kernel,
        out_shape=pltpu.VMEM((len(pieces), *pieces[0].shape[1:]), pieces[0].dtype),
        in_specs=[VMEM] * len(pieces),
        out_specs=VMEM,
        cost_estimate=pl.CostEstimate(flops=2**34, bytes_accessed=1000, transcendentals=0),
    )(*(pin(piece) for piece in pieces))


def finish_kernel(count, back_ref, far_ref, *refs):
    *near, cache_ref, stored_attention, attention_ref, sems = refs
    place = lax.axis_index("seq")
    rows = cache_ref.shape[3]
    request_rows = attention_ref.shape[0]
    width = back_ref.shape[2]
    parts = attention_ref.shape[1] // (count * width)
    riding = back_ref.shape[1] - parts * request_rows
    copies = []
    for j in range(count // 2):
        for d, piece in ((0, near[j].at[0]), (1, far_ref.at[j])):
            source = jnp.bitwise_xor(place, 2 * j + d)
            copies += [
                pltpu.make_async_copy(piece.at[:rows], cache_ref.at[0, 0, source], sems.at[2 * j + d, 0]),
                pltpu.make_async_copy(
                    piece.at[rows:], cache_ref.at[1, 0, source, : rows - riding], sems.at[2 * j + d, 1]
                ),
            ]
    copies.append(
        pltpu.make_async_copy(
            back_ref.at[:, parts * request_rows :], cache_ref.at[1, 0, :, rows - riding :], sems.at[0, 2]
        )
    )
    for copy in copies:
        copy.start()
    copies.append(pltpu.make_async_copy(attention_ref, stored_attention, sems.at[1, 2]))
    for s in range(count):
        block = back_ref[s, : parts * request_rows].astype(jnp.float32)
        for t in range(parts):
            attention_ref[:, (s * parts + t) * width : (s * parts + t + 1) * width] = block[
                t * request_rows : (t + 1) * request_rows
            ].astype(jnp.bfloat16)
    copies[-1].start()
    for copy in copies:
        copy.wait()


def local(new_kv, old_keys, old_values, suffix_keys, suffix_values, queries, lengths, assign):
    seq_count = lax.axis_size("seq")
    core_count = lax.axis_size("pd")
    if seq_count > KVH or seq_count & (seq_count - 1):
        return general(new_kv, old_keys, old_values, suffix_keys, suffix_values, queries, lengths, assign)
    half = seq_count // 2
    request_rows = queries.shape[0]
    prefix_rows = new_kv.shape[1]
    group_width = queries.shape[1] // seq_count
    width = new_kv.shape[2] // seq_count
    prefix_length = prefix_rows * seq_count * core_count // NPFX
    rates = pl.pallas_call(
        rates_kernel,
        out_shape=pltpu.VMEM((8, HD), jnp.float32),
        out_specs=VMEM,
        cost_estimate=pl.CostEstimate(flops=2**33, bytes_accessed=1000, transcendentals=0),
    )()
    queries, rates = lax.optimization_barrier((queries, rates))

    def swap(x, k):
        return lax.ppermute(x, "seq", [(i, i ^ k) for i in range(seq_count)])

    asked = lax.all_to_all(
        queries.reshape(request_rows, seq_count, group_width).transpose(1, 0, 2), "seq", 0, 0, tiled=True
    )
    early = (old_keys, suffix_keys, old_values)
    late = (suffix_values,)
    riding = 32
    piece = (2, 2 * prefix_rows - riding, width)
    packed = NQH // KVH * request_rows + riding
    *kv_cuts, ride = pl.pallas_call(
        functools.partial(prepare_kernel, seq_count, core_count, prefix_length, riding),
        out_shape=[pltpu.VMEM(piece, jnp.bfloat16)] * half + [pltpu.VMEM((seq_count, riding, width), jnp.bfloat16)],
        in_specs=[VMEM] * 2,
        out_specs=[VMEM] * (half + 1),
        cost_estimate=pl.CostEstimate(flops=2**33, bytes_accessed=1000, transcendentals=0),
        compiler_params=pltpu.CompilerParams(vmem_limit_bytes=16 * 2**20),
    )(pin(rates), pin(new_kv))
    kv_near = [kv_cuts[0]]
    for j in range(1, half):
        kv_near.append(swap(kv_cuts[j], 2 * j))
    attended = pl.pallas_call(
        functools.partial(attend_kernel, core_count),
        out_shape=pltpu.HBM((seq_count, packed, width), jnp.bfloat16),
        in_specs=[VMEM] + [HBM] * (2 + len(late)) + [VMEM] * (len(early) + 1),
        out_specs=HBM,
        scratch_shapes=[
            *(pltpu.VMEM(x.shape, x.dtype) for x in late),
            pltpu.VMEM((seq_count, packed - riding, width), jnp.bfloat16),
            pltpu.VMEM((1, assign.shape[0]), jnp.int32),
            pltpu.VMEM((1, assign.shape[0]), jnp.int32),
            pltpu.SemaphoreType.DMA((len(late), 4)),
            pltpu.SemaphoreType.DMA((4,)),
        ],
        compiler_params=pltpu.CompilerParams(vmem_limit_bytes=16 * 2**20),
        cost_estimate=pl.CostEstimate(flops=2**30, bytes_accessed=2**20, transcendentals=2**10),
    )(
        pin(asked),
        *(pin(x, pltpu.HBM) for x in (assign.reshape(1, -1), lengths.reshape(1, -1), *late)),
        *(pin(x) for x in early),
        pin(ride),
    )
    kv_far = swap(forward(kv_near), 1)
    back = lax.all_to_all(attended, "seq", 0, 0, tiled=True)
    return tuple(
        pl.pallas_call(
            functools.partial(finish_kernel, seq_count),
            out_shape=(
                jax.ShapeDtypeStruct((2, 1, seq_count, prefix_rows, width), jnp.bfloat16),
                jax.ShapeDtypeStruct((request_rows, NQH * HD), jnp.bfloat16),
            ),
            in_specs=[VMEM] * (half + 2),
            out_specs=(HBM, HBM),
            scratch_shapes=[
                pltpu.VMEM((request_rows, NQH * HD), jnp.bfloat16),
                pltpu.SemaphoreType.DMA((seq_count, 3)),
            ],
            cost_estimate=pl.CostEstimate(flops=0, bytes_accessed=2**20, transcendentals=0),
        )(*(pin(x) for x in (back, kv_far, *kv_near)))
    )


def solution(mesh):
    return jax.shard_map(
        local,
        mesh=mesh,
        in_specs=(
            P("grp", ("seq", "pd"), None),
            P("seq", "grp", None),
            P("seq", "grp", None),
            P("pd", "seq", "grp", None, None),
            P("pd", "seq", "grp", None, None),
            P(("seq", "pd"), "grp"),
            P("grp"),
            P("grp"),
        ),
        out_specs=(P(None, "seq", "grp", "pd", None), P(("seq", "pd"), "grp")),
        check_vma=False,
    )
```

```python
import functools
import math

import jax
import jax.numpy as jnp
from jax import lax
from jax.experimental import pallas as pl
from jax.experimental.pallas import tpu as pltpu
from jax.sharding import PartitionSpec as P

HD = 128
KVH = 16
NQH = 32
NPFX = 2


softcap = 50.0
query_scale = 1.0 / 12.0


def rotary(key_rows, positions):
    head_width = key_rows.shape[-1]
    halfway = head_width // 2
    inverse = 10000.0 ** (-2.0 * jnp.arange(halfway).astype(jnp.float32) / head_width)
    angles = positions.astype(jnp.float32)[:, None] * inverse[None, :]
    angles = jnp.concatenate([angles, angles], axis=1)
    values = key_rows.astype(jnp.float32)
    turned = jnp.concatenate([-values[..., halfway:], values[..., :halfway]], axis=-1)
    return values * jnp.cos(angles)[:, None, :] + turned * jnp.sin(angles)[:, None, :]


def capped(scores):
    return softcap * jnp.tanh(scores * query_scale / softcap)


def general(new_kv, old_keys, old_values, suffix_keys, suffix_values, queries, lengths, assign):
    seq_count = lax.axis_size("seq")
    core_count = lax.axis_size("pd")
    seq_place = lax.axis_index("seq")
    core_place = lax.axis_index("pd")
    per_kv = NQH // KVH
    sub_blocks = max(seq_count // KVH, 1)
    heads_here = max(KVH // seq_count, 1)
    head_groups = KVH // heads_here
    prefix_rows = new_kv.shape[1]
    request_rows = queries.shape[0]
    prefix_length = prefix_rows * seq_count * core_count // NPFX
    group_width = heads_here * per_kv * HD
    positions = (
        (seq_place * core_count + core_place) * prefix_rows
        + jnp.arange(prefix_rows, dtype=jnp.int32)
    ) % prefix_length
    rotated = rotary(new_kv[0].reshape(prefix_rows, KVH, HD), positions).astype(jnp.bfloat16)
    rotated = rotated.reshape(prefix_rows, KVH * HD)
    outgoing = jnp.stack([rotated, new_kv[1]]).reshape(
        2, prefix_rows // sub_blocks, seq_count, heads_here * HD
    )
    arrived = lax.all_to_all(outgoing, "seq", split_axis=2, concat_axis=1, tiled=True)
    new_cache = arrived.reshape(2, 1, seq_count, prefix_rows // sub_blocks, heads_here * HD)
    head_group = seq_place % head_groups
    token_block = seq_place // head_groups
    half_rows = seq_count * request_rows
    gathered = lax.all_gather(queries, "seq", axis=0, tiled=True)
    own_queries = lax.dynamic_slice_in_dim(gathered, head_group * group_width, group_width, 1)
    query_blocks = own_queries.reshape(half_rows, heads_here, per_kv, HD)
    own_assign = lax.dynamic_index_in_dim(
        assign.reshape(seq_count, core_count, request_rows), core_place, 1, keepdims=False
    ).reshape(half_rows)
    own_lengths = lax.dynamic_index_in_dim(
        lengths.reshape(seq_count, core_count, request_rows), core_place, 1, keepdims=False
    ).reshape(half_rows)
    prefix_keys = old_keys[0].reshape(-1, heads_here, HD)
    prefix_values = old_values[0].reshape(-1, heads_here, HD)
    token_count = prefix_keys.shape[0]
    token_prefix = (
        jnp.arange(token_count, dtype=jnp.int32) * sub_blocks + token_block
    ) // prefix_length
    block_rows = math.gcd(half_rows, 256)

    def prefix_block(block_index):
        row_start = block_index * block_rows
        query_part = lax.dynamic_slice_in_dim(query_blocks, row_start, block_rows, 0)
        assign_part = lax.dynamic_slice_in_dim(own_assign, row_start, block_rows, 0)
        scores = capped(
            jnp.einsum(
                "rhqd,thd->rhqt", query_part, prefix_keys, preferred_element_type=jnp.float32
            )
        )
        allowed = (assign_part[:, None] == token_prefix[None, :])[:, None, None, :]
        weights = jnp.where(allowed, jnp.exp(scores), 0.0)
        totals = jnp.sum(weights, axis=-1)
        numerators = jnp.einsum(
            "rhqt,thd->rhqd",
            weights.astype(jnp.bfloat16),
            prefix_values,
            preferred_element_type=jnp.float32,
        )
        return (totals, numerators)

    totals, numerators = lax.map(prefix_block, jnp.arange(half_rows // block_rows, dtype=jnp.int32))
    totals = totals.reshape(half_rows, heads_here, per_kv)
    numerators = numerators.reshape(half_rows, heads_here, per_kv, HD)
    suffix_rows = head_groups * request_rows
    suffix_start = token_block * suffix_rows
    suffix_query = lax.dynamic_slice_in_dim(query_blocks, suffix_start, suffix_rows, 0)
    suffix_length = lax.dynamic_slice_in_dim(own_lengths, suffix_start, suffix_rows, 0)
    recent_keys = suffix_keys[0, 0].reshape(suffix_rows, -1, heads_here, HD)
    recent_values = suffix_values[0, 0].reshape(suffix_rows, -1, heads_here, HD)
    recent_scores = capped(
        jnp.einsum("rhqd,rphd->rhqp", suffix_query, recent_keys, preferred_element_type=jnp.float32)
    )
    live_slots = jnp.arange(recent_keys.shape[1], dtype=jnp.int32)[None, :] < suffix_length[:, None]
    recent_weights = jnp.where(live_slots[:, None, None, :], jnp.exp(recent_scores), 0.0)
    recent_totals = jnp.sum(recent_weights, axis=-1)
    recent_numerators = jnp.einsum(
        "rhqp,rphd->rhqd",
        recent_weights.astype(jnp.bfloat16),
        recent_values,
        preferred_element_type=jnp.float32,
    )
    totals = lax.dynamic_update_slice_in_dim(
        totals,
        lax.dynamic_slice_in_dim(totals, suffix_start, suffix_rows, 0) + recent_totals,
        suffix_start,
        0,
    )
    numerators = lax.dynamic_update_slice_in_dim(
        numerators,
        lax.dynamic_slice_in_dim(numerators, suffix_start, suffix_rows, 0) + recent_numerators,
        suffix_start,
        0,
    )
    back_numerators, back_totals = (
        lax.all_to_all(
            numerators.reshape(seq_count, request_rows, group_width),
            "seq",
            split_axis=0,
            concat_axis=0,
            tiled=True,
        ),
        lax.all_to_all(
            totals.reshape(seq_count, request_rows, heads_here * per_kv),
            "seq",
            split_axis=0,
            concat_axis=0,
            tiled=True,
        ),
    )
    back_numerators = back_numerators.reshape(
        sub_blocks, head_groups, request_rows, heads_here * per_kv, HD
    ).sum(0)
    back_totals = back_totals.reshape(
        sub_blocks, head_groups, request_rows, heads_here * per_kv
    ).sum(0)
    attention = (
        (back_numerators / back_totals[..., None])
        .transpose(1, 0, 2, 3)
        .reshape(request_rows, NQH * HD)
    )
    return (new_cache, attention.astype(jnp.bfloat16))


def weigh(scores):
    return jnp.exp2((softcap * math.log2(math.e)) * jnp.tanh(scores * (query_scale / softcap)))


NT = (((1,), (1,)), ((), ()))
NN = (((1,), (0,)), ((), ()))


def pin(x, space=pltpu.VMEM):
    return pltpu.with_memory_space_constraint(x, space)


VMEM = pl.BlockSpec(memory_space=pltpu.VMEM)
HBM = pl.BlockSpec(memory_space=pltpu.HBM)


def own_column(values_ref, tall, request_rows, core_count):
    shape = (tall, values_ref.shape[1])
    row = lax.broadcasted_iota(jnp.int32, shape, 0) % (values_ref.shape[1] // core_count)
    wanted = (row // request_rows * core_count + lax.axis_index("pd")) * request_rows + row % request_rows
    picked = jnp.where(lax.broadcasted_iota(jnp.int32, shape, 1) == wanted, values_ref[...], 0)
    return jnp.sum(picked.astype(jnp.float32), axis=1, keepdims=True).astype(jnp.int32)


def rates_kernel(rates_ref):
    step = lax.broadcasted_iota(jnp.int32, rates_ref.shape, 1) % (HD // 2)
    rates_ref[...] = jnp.exp2(step.astype(jnp.float32) * (-2.0 / HD * math.log2(10000.0)))


def prepare_kernel(count, core_count, prefix_length, riding, rates_ref, kv_ref, *refs):
    *pieces, ride_ref = refs
    place = lax.axis_index("seq")
    rows = kv_ref.shape[1]
    width = kv_ref.shape[2] // count
    first = (place * core_count + lax.axis_index("pd")) * rows
    position = (first + lax.broadcasted_iota(jnp.int32, (rows, HD), 0)) % prefix_length
    angles = position.astype(jnp.float32) * rates_ref[:1]
    cosine = jnp.cos(angles)
    sine = jnp.sin(angles)
    sine = jnp.where(lax.broadcasted_iota(jnp.int32, (rows, HD), 1) < HD // 2, -sine, sine)
    for j in reversed(range(count // 2)):
        for d in range(2):
            start = jnp.bitwise_xor(place, 2 * j + d) * width
            for h in range(width // HD):
                columns = pl.ds(pl.multiple_of(start + h * HD, HD), HD)
                keys = kv_ref[0, :, columns].astype(jnp.float32)
                turned = pltpu.roll(keys, HD // 2, 1)
                pieces[j][d, :rows, h * HD : (h + 1) * HD] = (keys * cosine + turned * sine).astype(jnp.bfloat16)
                pieces[j][d, rows:, h * HD : (h + 1) * HD] = kv_ref[1, : rows - riding, columns]
    for s in range(count):
        ride_ref[s] = kv_ref[1, rows - riding :, s * width : (s + 1) * width]


def fetch(stored, target, sems):
    parts = sems.shape[0]
    leading = stored.shape[:-3] if len(stored.shape) > 3 else stored.shape[:1]
    index = (0,) * len(leading)
    rows = stored.shape[len(leading)] // parts
    copies = []
    for i in range(parts):
        at = (*index, pl.ds(i * rows, rows))
        copies.append(pltpu.make_async_copy(stored.at[at], target.at[at], sems.at[i]))
        copies[-1].start()
    return copies


def attend_kernel(
    core_count, q_ref, stored_assign, stored_lengths, stored_svalues,
    keys_ref, skeys_ref, values_ref, ride_ref, stored_out, svalues_ref, out_ref, assign_ref, lengths_ref, sems, out_sems,
):
    small = [
        pltpu.make_async_copy(stored_assign, assign_ref, out_sems.at[2]),
        pltpu.make_async_copy(stored_lengths, lengths_ref, out_sems.at[3]),
    ]
    for copy in small:
        copy.start()
    fetches = [
        fetch(a, b, sems.at[i]) for i, (a, b) in enumerate(((stored_svalues, svalues_ref),))
    ]
    seq_count, span, group_width = q_ref.shape
    requests = seq_count * span
    per_kv = NQH // KVH
    width = keys_ref.shape[2]
    heads_here = width // HD
    length = keys_ref.shape[1] // NPFX
    slots = skeys_ref.shape[3]
    queries = q_ref[...].reshape(requests, group_width)
    heads = [(h, j) for h in range(heads_here) for j in range(per_kv)]
    query = {(h, j): queries[:, (h * per_kv + j) * HD : (h * per_kv + j + 1) * HD] for h, j in heads}
    query32 = {key: value.astype(jnp.float32) for key, value in query.items()}
    blank = jnp.zeros((span, HD), jnp.float32)
    tall = span * len(heads)
    column = lax.broadcasted_iota(jnp.int32, (tall, span * slots), 1)
    low = lax.broadcasted_iota(jnp.int32, (tall, span * slots), 0) % span * slots
    ride = pltpu.make_async_copy(ride_ref, stored_out.at[:, per_kv * span :], out_sems.at[0])
    ride.start()
    blocks = [slice(b * span, (b + 1) * span) for b in range(seq_count)]
    found = []
    for rows in blocks:
        part = jnp.concatenate(
            [
                jnp.concatenate([query32[h, j][rows] if g == h else blank for g in range(heads_here)], axis=1)
                for h, j in heads
            ],
            axis=0,
        ).astype(jnp.bfloat16)
        skeys = skeys_ref[0, 0, rows].reshape(span * slots, width)
        found.append(lax.dot_general(part, skeys, NT, preferred_element_type=jnp.float32))
    for copy in small:
        copy.wait()
    which = own_column(assign_ref, per_kv * requests, span, core_count)
    live = own_column(lengths_ref, requests, span, core_count)
    added, more = {}, {}
    for b, rows in enumerate(blocks):
        slots_live = jnp.concatenate([live[rows]] * len(heads), axis=0)
        weights = jnp.where((column >= low) & (column < low + slots_live), weigh(found[b]), 0.0)
        sums = jnp.sum(weights, axis=1, keepdims=True)
        for i, (h, j) in enumerate(heads):
            more[h, j, b] = sums[i * span : (i + 1) * span]
        found[b] = weights.astype(jnp.bfloat16)
    numerators, totals = [], []
    for h in range(heads_here):
        columns = slice(h * HD, (h + 1) * HD)
        stacked = jnp.concatenate([query[h, j] for j in range(per_kv)], axis=0)
        scores = lax.dot_general(stacked, keys_ref[0, :length, columns], NT, preferred_element_type=jnp.float32)
        for p in range(1, NPFX):
            other = lax.dot_general(
                stacked, keys_ref[0, p * length : (p + 1) * length, columns], NT, preferred_element_type=jnp.float32
            )
            scores = jnp.where(which == p, other, scores)
        weights = weigh(scores)
        totals.append(jnp.sum(weights, axis=1, keepdims=True))
        rounded = weights.astype(jnp.bfloat16)
        numerator = jnp.dot(rounded, values_ref[0, :length, columns], preferred_element_type=jnp.float32)
        for p in range(1, NPFX):
            other = jnp.dot(
                rounded, values_ref[0, p * length : (p + 1) * length, columns], preferred_element_type=jnp.float32
            )
            numerator = jnp.where(which == p, other, numerator)
        numerators.append(numerator)
    for copy in fetches[0]:
        copy.wait()
    for b, rows in enumerate(blocks):
        svalues = svalues_ref[0, 0, rows].reshape(span * slots, width)
        products = jnp.dot(found[b], svalues, preferred_element_type=jnp.float32)
        for i, (h, j) in enumerate(heads):
            added[h, j, b] = products[i * span : (i + 1) * span, h * HD : (h + 1) * HD]
    results = []
    for h in range(heads_here):

        def regroup(cut):
            return jnp.concatenate([cut[h, j, b] for j in range(per_kv) for b in range(seq_count)], axis=0)

        result = (numerators[h] + regroup(added)) * (1.0 / (totals[h] + regroup(more)))
        for j in range(per_kv):
            results.append(result[j * requests : (j + 1) * requests].reshape(seq_count, span, HD))
    for c in range(heads_here):
        out_ref[:, :, c * HD : (c + 1) * HD] = jnp.concatenate(
            [results[t * heads_here + c] for t in range(per_kv)], axis=1
        ).astype(jnp.bfloat16)
    out = pltpu.make_async_copy(out_ref, stored_out.at[:, : per_kv * span], out_sems.at[1])
    out.start()
    ride.wait()
    out.wait()


def forward_kernel(*refs):
    *pieces, out_ref = refs
    for j, piece in enumerate(pieces):
        out_ref[j] = piece[1]


def forward(pieces):
    return pl.pallas_call(
        forward_kernel,
        out_shape=pltpu.VMEM((len(pieces), *pieces[0].shape[1:]), pieces[0].dtype),
        in_specs=[VMEM] * len(pieces),
        out_specs=VMEM,
        cost_estimate=pl.CostEstimate(flops=2**34, bytes_accessed=1000, transcendentals=0),
    )(*(pin(piece) for piece in pieces))


def cache_kernel(count, far_ref, *refs):
    *near, cache_ref, sems = refs
    place = lax.axis_index("seq")
    rows = cache_ref.shape[3]
    kept = far_ref.shape[1] - rows
    copies = []
    for j in range(count // 2):
        for d, piece in ((0, near[j].at[0]), (1, far_ref.at[j])):
            source = jnp.bitwise_xor(place, 2 * j + d)
            copies += [
                pltpu.make_async_copy(piece.at[:rows], cache_ref.at[0, 0, source], sems.at[2 * j + d, 0]),
                pltpu.make_async_copy(piece.at[rows:], cache_ref.at[1, 0, source, :kept], sems.at[2 * j + d, 1]),
            ]
    for copy in copies:
        copy.start()
    for copy in copies:
        copy.wait()


def finish_kernel(back_ref, _, cache_ref, stored_attention, attention_ref, sems):
    count, packed, width = back_ref.shape
    rows = cache_ref.shape[3]
    request_rows = attention_ref.shape[0]
    parts = attention_ref.shape[1] // (count * width)
    kept = rows - (packed - parts * request_rows)
    ride = pltpu.make_async_copy(
        back_ref.at[:, parts * request_rows :], cache_ref.at[1, 0, :, kept:], sems.at[0]
    )
    ride.start()
    for s in range(count):
        block = back_ref[s, : parts * request_rows].astype(jnp.float32)
        for t in range(parts):
            attention_ref[:, (s * parts + t) * width : (s * parts + t + 1) * width] = block[
                t * request_rows : (t + 1) * request_rows
            ].astype(jnp.bfloat16)
    out = pltpu.make_async_copy(attention_ref, stored_attention, sems.at[1])
    out.start()
    ride.wait()
    out.wait()


def local(new_kv, old_keys, old_values, suffix_keys, suffix_values, queries, lengths, assign):
    seq_count = lax.axis_size("seq")
    core_count = lax.axis_size("pd")
    if seq_count > KVH or seq_count & (seq_count - 1):
        return general(new_kv, old_keys, old_values, suffix_keys, suffix_values, queries, lengths, assign)
    half = seq_count // 2
    request_rows = queries.shape[0]
    prefix_rows = new_kv.shape[1]
    group_width = queries.shape[1] // seq_count
    width = new_kv.shape[2] // seq_count
    prefix_length = prefix_rows * seq_count * core_count // NPFX
    rates = pl.pallas_call(
        rates_kernel,
        out_shape=pltpu.VMEM((8, HD), jnp.float32),
        out_specs=VMEM,
        cost_estimate=pl.CostEstimate(flops=2**33, bytes_accessed=1000, transcendentals=0),
    )()
    queries, rates = lax.optimization_barrier((queries, rates))

    def swap(x, k):
        return lax.ppermute(x, "seq", [(i, i ^ k) for i in range(seq_count)])

    asked = lax.all_to_all(
        queries.reshape(request_rows, seq_count, group_width).transpose(1, 0, 2), "seq", 0, 0, tiled=True
    )
    early = (old_keys, suffix_keys, old_values)
    late = (suffix_values,)
    riding = 32
    piece = (2, 2 * prefix_rows - riding, width)
    packed = NQH // KVH * request_rows + riding
    *kv_cuts, ride = pl.pallas_call(
        functools.partial(prepare_kernel, seq_count, core_count, prefix_length, riding),
        out_shape=[pltpu.VMEM(piece, jnp.bfloat16)] * half + [pltpu.VMEM((seq_count, riding, width), jnp.bfloat16)],
        in_specs=[VMEM] * 2,
        out_specs=[VMEM] * (half + 1),
        cost_estimate=pl.CostEstimate(flops=2**33, bytes_accessed=1000, transcendentals=0),
        compiler_params=pltpu.CompilerParams(vmem_limit_bytes=16 * 2**20),
    )(pin(rates), pin(new_kv))
    kv_near = [kv_cuts[0]]
    for j in range(1, half):
        kv_near.append(swap(kv_cuts[j], 2 * j))
    attended = pl.pallas_call(
        functools.partial(attend_kernel, core_count),
        out_shape=pltpu.HBM((seq_count, packed, width), jnp.bfloat16),
        in_specs=[VMEM] + [HBM] * (2 + len(late)) + [VMEM] * (len(early) + 1),
        out_specs=HBM,
        scratch_shapes=[
            *(pltpu.VMEM(x.shape, x.dtype) for x in late),
            pltpu.VMEM((seq_count, packed - riding, width), jnp.bfloat16),
            pltpu.VMEM((1, assign.shape[0]), jnp.int32),
            pltpu.VMEM((1, assign.shape[0]), jnp.int32),
            pltpu.SemaphoreType.DMA((len(late), 4)),
            pltpu.SemaphoreType.DMA((4,)),
        ],
        compiler_params=pltpu.CompilerParams(vmem_limit_bytes=16 * 2**20),
        cost_estimate=pl.CostEstimate(flops=2**30, bytes_accessed=2**20, transcendentals=2**10),
    )(
        pin(asked),
        *(pin(x, pltpu.HBM) for x in (assign.reshape(1, -1), lengths.reshape(1, -1), *late)),
        *(pin(x) for x in early),
        pin(ride),
    )
    kv_far = swap(forward(kv_near), 1)
    back = lax.all_to_all(attended, "seq", 0, 0, tiled=True)
    cache_shape = (2, 1, seq_count, prefix_rows, width)
    cache = pl.pallas_call(
        functools.partial(cache_kernel, seq_count),
        out_shape=pltpu.HBM(cache_shape, jnp.bfloat16),
        in_specs=[VMEM] * (half + 1),
        out_specs=HBM,
        scratch_shapes=[pltpu.SemaphoreType.DMA((seq_count, 2))],
        cost_estimate=pl.CostEstimate(flops=2**30, bytes_accessed=2**20, transcendentals=0),
    )(*(pin(x) for x in (kv_far, *kv_near)))
    return tuple(
        pl.pallas_call(
            finish_kernel,
            out_shape=(
                pltpu.HBM(cache_shape, jnp.bfloat16),
                pltpu.HBM((request_rows, NQH * HD), jnp.bfloat16),
            ),
            in_specs=[VMEM, HBM],
            out_specs=(HBM, HBM),
            scratch_shapes=[
                pltpu.VMEM((request_rows, NQH * HD), jnp.bfloat16),
                pltpu.SemaphoreType.DMA((2,)),
            ],
            input_output_aliases={1: 0},
            cost_estimate=pl.CostEstimate(flops=0, bytes_accessed=2**20, transcendentals=0),
        )(pin(back), cache)
    )


def solution(mesh):
    return jax.shard_map(
        local,
        mesh=mesh,
        in_specs=(
            P("grp", ("seq", "pd"), None),
            P("seq", "grp", None),
            P("seq", "grp", None),
            P("pd", "seq", "grp", None, None),
            P("pd", "seq", "grp", None, None),
            P(("seq", "pd"), "grp"),
            P("grp"),
            P("grp"),
        ),
        out_specs=(P(None, "seq", "grp", "pd", None), P(("seq", "pd"), "grp")),
        check_vma=False,
    )
```

```python
import functools
import math

import jax
import jax.numpy as jnp
from jax import lax
from jax.experimental import pallas as pl
from jax.experimental.pallas import tpu as pltpu
from jax.sharding import PartitionSpec as P

HD = 128
KVH = 16
NQH = 32
NPFX = 2


softcap = 50.0
query_scale = 1.0 / 12.0


def rotary(key_rows, positions):
    head_width = key_rows.shape[-1]
    halfway = head_width // 2
    inverse = 10000.0 ** (-2.0 * jnp.arange(halfway).astype(jnp.float32) / head_width)
    angles = positions.astype(jnp.float32)[:, None] * inverse[None, :]
    angles = jnp.concatenate([angles, angles], axis=1)
    values = key_rows.astype(jnp.float32)
    turned = jnp.concatenate([-values[..., halfway:], values[..., :halfway]], axis=-1)
    return values * jnp.cos(angles)[:, None, :] + turned * jnp.sin(angles)[:, None, :]


def capped(scores):
    return softcap * jnp.tanh(scores * query_scale / softcap)


def general(new_kv, old_keys, old_values, suffix_keys, suffix_values, queries, lengths, assign):
    seq_count = lax.axis_size("seq")
    core_count = lax.axis_size("pd")
    seq_place = lax.axis_index("seq")
    core_place = lax.axis_index("pd")
    per_kv = NQH // KVH
    sub_blocks = max(seq_count // KVH, 1)
    heads_here = max(KVH // seq_count, 1)
    head_groups = KVH // heads_here
    prefix_rows = new_kv.shape[1]
    request_rows = queries.shape[0]
    prefix_length = prefix_rows * seq_count * core_count // NPFX
    group_width = heads_here * per_kv * HD
    positions = (
        (seq_place * core_count + core_place) * prefix_rows
        + jnp.arange(prefix_rows, dtype=jnp.int32)
    ) % prefix_length
    rotated = rotary(new_kv[0].reshape(prefix_rows, KVH, HD), positions).astype(jnp.bfloat16)
    rotated = rotated.reshape(prefix_rows, KVH * HD)
    outgoing = jnp.stack([rotated, new_kv[1]]).reshape(
        2, prefix_rows // sub_blocks, seq_count, heads_here * HD
    )
    arrived = lax.all_to_all(outgoing, "seq", split_axis=2, concat_axis=1, tiled=True)
    new_cache = arrived.reshape(2, 1, seq_count, prefix_rows // sub_blocks, heads_here * HD)
    head_group = seq_place % head_groups
    token_block = seq_place // head_groups
    half_rows = seq_count * request_rows
    gathered = lax.all_gather(queries, "seq", axis=0, tiled=True)
    own_queries = lax.dynamic_slice_in_dim(gathered, head_group * group_width, group_width, 1)
    query_blocks = own_queries.reshape(half_rows, heads_here, per_kv, HD)
    own_assign = lax.dynamic_index_in_dim(
        assign.reshape(seq_count, core_count, request_rows), core_place, 1, keepdims=False
    ).reshape(half_rows)
    own_lengths = lax.dynamic_index_in_dim(
        lengths.reshape(seq_count, core_count, request_rows), core_place, 1, keepdims=False
    ).reshape(half_rows)
    prefix_keys = old_keys[0].reshape(-1, heads_here, HD)
    prefix_values = old_values[0].reshape(-1, heads_here, HD)
    token_count = prefix_keys.shape[0]
    token_prefix = (
        jnp.arange(token_count, dtype=jnp.int32) * sub_blocks + token_block
    ) // prefix_length
    block_rows = math.gcd(half_rows, 256)

    def prefix_block(block_index):
        row_start = block_index * block_rows
        query_part = lax.dynamic_slice_in_dim(query_blocks, row_start, block_rows, 0)
        assign_part = lax.dynamic_slice_in_dim(own_assign, row_start, block_rows, 0)
        scores = capped(
            jnp.einsum(
                "rhqd,thd->rhqt", query_part, prefix_keys, preferred_element_type=jnp.float32
            )
        )
        allowed = (assign_part[:, None] == token_prefix[None, :])[:, None, None, :]
        weights = jnp.where(allowed, jnp.exp(scores), 0.0)
        totals = jnp.sum(weights, axis=-1)
        numerators = jnp.einsum(
            "rhqt,thd->rhqd",
            weights.astype(jnp.bfloat16),
            prefix_values,
            preferred_element_type=jnp.float32,
        )
        return (totals, numerators)

    totals, numerators = lax.map(prefix_block, jnp.arange(half_rows // block_rows, dtype=jnp.int32))
    totals = totals.reshape(half_rows, heads_here, per_kv)
    numerators = numerators.reshape(half_rows, heads_here, per_kv, HD)
    suffix_rows = head_groups * request_rows
    suffix_start = token_block * suffix_rows
    suffix_query = lax.dynamic_slice_in_dim(query_blocks, suffix_start, suffix_rows, 0)
    suffix_length = lax.dynamic_slice_in_dim(own_lengths, suffix_start, suffix_rows, 0)
    recent_keys = suffix_keys[0, 0].reshape(suffix_rows, -1, heads_here, HD)
    recent_values = suffix_values[0, 0].reshape(suffix_rows, -1, heads_here, HD)
    recent_scores = capped(
        jnp.einsum("rhqd,rphd->rhqp", suffix_query, recent_keys, preferred_element_type=jnp.float32)
    )
    live_slots = jnp.arange(recent_keys.shape[1], dtype=jnp.int32)[None, :] < suffix_length[:, None]
    recent_weights = jnp.where(live_slots[:, None, None, :], jnp.exp(recent_scores), 0.0)
    recent_totals = jnp.sum(recent_weights, axis=-1)
    recent_numerators = jnp.einsum(
        "rhqp,rphd->rhqd",
        recent_weights.astype(jnp.bfloat16),
        recent_values,
        preferred_element_type=jnp.float32,
    )
    totals = lax.dynamic_update_slice_in_dim(
        totals,
        lax.dynamic_slice_in_dim(totals, suffix_start, suffix_rows, 0) + recent_totals,
        suffix_start,
        0,
    )
    numerators = lax.dynamic_update_slice_in_dim(
        numerators,
        lax.dynamic_slice_in_dim(numerators, suffix_start, suffix_rows, 0) + recent_numerators,
        suffix_start,
        0,
    )
    back_numerators, back_totals = (
        lax.all_to_all(
            numerators.reshape(seq_count, request_rows, group_width),
            "seq",
            split_axis=0,
            concat_axis=0,
            tiled=True,
        ),
        lax.all_to_all(
            totals.reshape(seq_count, request_rows, heads_here * per_kv),
            "seq",
            split_axis=0,
            concat_axis=0,
            tiled=True,
        ),
    )
    back_numerators = back_numerators.reshape(
        sub_blocks, head_groups, request_rows, heads_here * per_kv, HD
    ).sum(0)
    back_totals = back_totals.reshape(
        sub_blocks, head_groups, request_rows, heads_here * per_kv
    ).sum(0)
    attention = (
        (back_numerators / back_totals[..., None])
        .transpose(1, 0, 2, 3)
        .reshape(request_rows, NQH * HD)
    )
    return (new_cache, attention.astype(jnp.bfloat16))


def weigh(scores):
    return jnp.exp2((softcap * math.log2(math.e)) * jnp.tanh(scores * (query_scale / softcap)))


NT = (((1,), (1,)), ((), ()))
NN = (((1,), (0,)), ((), ()))


def pin(x, space=pltpu.VMEM):
    return pltpu.with_memory_space_constraint(x, space)


VMEM = pl.BlockSpec(memory_space=pltpu.VMEM)
HBM = pl.BlockSpec(memory_space=pltpu.HBM)


def own_column(values_ref, tall, request_rows, core_count):
    shape = (tall, values_ref.shape[1])
    row = lax.broadcasted_iota(jnp.int32, shape, 0) % (values_ref.shape[1] // core_count)
    wanted = (row // request_rows * core_count + lax.axis_index("pd")) * request_rows + row % request_rows
    picked = jnp.where(lax.broadcasted_iota(jnp.int32, shape, 1) == wanted, values_ref[...], 0)
    return jnp.sum(picked.astype(jnp.float32), axis=1, keepdims=True).astype(jnp.int32)


def rates_kernel(rates_ref):
    step = lax.broadcasted_iota(jnp.int32, rates_ref.shape, 1) % (HD // 2)
    rates_ref[...] = jnp.exp2(step.astype(jnp.float32) * (-2.0 / HD * math.log2(10000.0)))


def prepare_kernel(count, core_count, prefix_length, riding, rates_ref, kv_ref, *refs):
    *pieces, ride_ref = refs
    place = lax.axis_index("seq")
    rows = kv_ref.shape[1]
    width = kv_ref.shape[2] // count
    first = (place * core_count + lax.axis_index("pd")) * rows
    position = (first + lax.broadcasted_iota(jnp.int32, (rows, HD), 0)) % prefix_length
    angles = position.astype(jnp.float32) * rates_ref[:1]
    cosine = jnp.cos(angles)
    sine = jnp.sin(angles)
    sine = jnp.where(lax.broadcasted_iota(jnp.int32, (rows, HD), 1) < HD // 2, -sine, sine)
    for j in reversed(range(count // 2)):
        for d in range(2):
            start = jnp.bitwise_xor(place, 2 * j + d) * width
            for h in range(width // HD):
                columns = pl.ds(pl.multiple_of(start + h * HD, HD), HD)
                keys = kv_ref[0, :, columns].astype(jnp.float32)
                turned = pltpu.roll(keys, HD // 2, 1)
                pieces[j][d, :rows, h * HD : (h + 1) * HD] = (keys * cosine + turned * sine).astype(jnp.bfloat16)
                pieces[j][d, rows:, h * HD : (h + 1) * HD] = kv_ref[1, : rows - riding, columns]
    for s in range(count):
        ride_ref[s] = kv_ref[1, rows - riding :, s * width : (s + 1) * width]


def fetch(stored, target, sems):
    parts = sems.shape[0]
    leading = stored.shape[:-3] if len(stored.shape) > 3 else stored.shape[:1]
    index = (0,) * len(leading)
    rows = stored.shape[len(leading)] // parts
    copies = []
    for i in range(parts):
        at = (*index, pl.ds(i * rows, rows))
        copies.append(pltpu.make_async_copy(stored.at[at], target.at[at], sems.at[i]))
        copies[-1].start()
    return copies


def attend_kernel(
    core_count, q_ref, stored_assign, stored_lengths, stored_svalues,
    keys_ref, skeys_ref, values_ref, ride_ref, stored_out, svalues_ref, out_ref, assign_ref, lengths_ref, sems, out_sems,
):
    small = [
        pltpu.make_async_copy(stored_assign, assign_ref, out_sems.at[2]),
        pltpu.make_async_copy(stored_lengths, lengths_ref, out_sems.at[3]),
    ]
    for copy in small:
        copy.start()
    fetches = [
        fetch(a, b, sems.at[i]) for i, (a, b) in enumerate(((stored_svalues, svalues_ref),))
    ]
    seq_count, span, group_width = q_ref.shape
    requests = seq_count * span
    per_kv = NQH // KVH
    width = keys_ref.shape[2]
    heads_here = width // HD
    length = keys_ref.shape[1] // NPFX
    slots = skeys_ref.shape[3]
    queries = q_ref[...].reshape(requests, group_width)
    heads = [(h, j) for h in range(heads_here) for j in range(per_kv)]
    query = {(h, j): queries[:, (h * per_kv + j) * HD : (h * per_kv + j + 1) * HD] for h, j in heads}
    query32 = {key: value.astype(jnp.float32) for key, value in query.items()}
    blank = jnp.zeros((span, HD), jnp.float32)
    tall = span * len(heads)
    column = lax.broadcasted_iota(jnp.int32, (tall, span * slots), 1)
    low = lax.broadcasted_iota(jnp.int32, (tall, span * slots), 0) % span * slots
    ride = pltpu.make_async_copy(ride_ref, stored_out.at[:, per_kv * span :], out_sems.at[0])
    ride.start()
    blocks = [slice(b * span, (b + 1) * span) for b in range(seq_count)]
    found = []
    for rows in blocks:
        part = jnp.concatenate(
            [
                jnp.concatenate([query32[h, j][rows] if g == h else blank for g in range(heads_here)], axis=1)
                for h, j in heads
            ],
            axis=0,
        ).astype(jnp.bfloat16)
        skeys = skeys_ref[0, 0, rows].reshape(span * slots, width)
        found.append(lax.dot_general(part, skeys, NT, preferred_element_type=jnp.float32))
    for copy in small:
        copy.wait()
    which = own_column(assign_ref, per_kv * requests, span, core_count)
    live = own_column(lengths_ref, requests, span, core_count)
    added, more = {}, {}
    for b, rows in enumerate(blocks):
        slots_live = jnp.concatenate([live[rows]] * len(heads), axis=0)
        weights = jnp.where((column >= low) & (column < low + slots_live), weigh(found[b]), 0.0)
        sums = jnp.sum(weights, axis=1, keepdims=True)
        for i, (h, j) in enumerate(heads):
            more[h, j, b] = sums[i * span : (i + 1) * span]
        found[b] = weights.astype(jnp.bfloat16)
    numerators, totals = [], []
    for h in range(heads_here):
        columns = slice(h * HD, (h + 1) * HD)
        stacked = jnp.concatenate([query[h, j] for j in range(per_kv)], axis=0)
        scores = lax.dot_general(stacked, keys_ref[0, :length, columns], NT, preferred_element_type=jnp.float32)
        for p in range(1, NPFX):
            other = lax.dot_general(
                stacked, keys_ref[0, p * length : (p + 1) * length, columns], NT, preferred_element_type=jnp.float32
            )
            scores = jnp.where(which == p, other, scores)
        weights = weigh(scores)
        totals.append(jnp.sum(weights, axis=1, keepdims=True))
        rounded = weights.astype(jnp.bfloat16)
        numerator = jnp.dot(rounded, values_ref[0, :length, columns], preferred_element_type=jnp.float32)
        for p in range(1, NPFX):
            other = jnp.dot(
                rounded, values_ref[0, p * length : (p + 1) * length, columns], preferred_element_type=jnp.float32
            )
            numerator = jnp.where(which == p, other, numerator)
        numerators.append(numerator)
    for copy in fetches[0]:
        copy.wait()
    for b, rows in enumerate(blocks):
        svalues = svalues_ref[0, 0, rows].reshape(span * slots, width)
        products = jnp.dot(found[b], svalues, preferred_element_type=jnp.float32)
        for i, (h, j) in enumerate(heads):
            added[h, j, b] = products[i * span : (i + 1) * span, h * HD : (h + 1) * HD]
    results = []
    for h in range(heads_here):

        def regroup(cut):
            return jnp.concatenate([cut[h, j, b] for j in range(per_kv) for b in range(seq_count)], axis=0)

        result = (numerators[h] + regroup(added)) * (1.0 / (totals[h] + regroup(more)))
        for j in range(per_kv):
            results.append(result[j * requests : (j + 1) * requests].reshape(seq_count, span, HD))
    for c in range(heads_here):
        out_ref[:, :, c * HD : (c + 1) * HD] = jnp.concatenate(
            [results[t * heads_here + c] for t in range(per_kv)], axis=1
        ).astype(jnp.bfloat16)
    out = pltpu.make_async_copy(out_ref, stored_out.at[:, : per_kv * span], out_sems.at[1])
    out.start()
    ride.wait()
    out.wait()


def forward_kernel(*refs):
    *pieces, out_ref = refs
    for j, piece in enumerate(pieces):
        out_ref[j] = piece[1]


def forward(pieces):
    return pl.pallas_call(
        forward_kernel,
        out_shape=pltpu.VMEM((len(pieces), *pieces[0].shape[1:]), pieces[0].dtype),
        in_specs=[VMEM] * len(pieces),
        out_specs=VMEM,
        cost_estimate=pl.CostEstimate(flops=2**34, bytes_accessed=1000, transcendentals=0),
    )(*(pin(piece) for piece in pieces))


def place_blocks(blocks, cache_ref, sems):
    rows = cache_ref.shape[3]
    copies = []
    for i, (source, piece) in enumerate(blocks):
        kept = piece.shape[0] - rows
        copies += [
            pltpu.make_async_copy(piece.at[:rows], cache_ref.at[0, 0, source], sems.at[i, 0]),
            pltpu.make_async_copy(piece.at[rows:], cache_ref.at[1, 0, source, :kept], sems.at[i, 1]),
        ]
    for copy in copies:
        copy.start()
    for copy in copies:
        copy.wait()


def near_kernel(count, *refs):
    *near, cache_ref, sems = refs
    place = lax.axis_index("seq")
    place_blocks(
        [(jnp.bitwise_xor(place, 2 * j), near[i].at[0]) for i, j in enumerate(range(count // 2))], cache_ref, sems
    )


def far_kernel(count, far_ref, _, cache_ref, sems):
    place = lax.axis_index("seq")
    place_blocks(
        [(jnp.bitwise_xor(place, 2 * j + 1), far_ref.at[j]) for j in range(count // 2)], cache_ref, sems
    )


def finish_kernel(back_ref, _, cache_ref, stored_attention, attention_ref, sems):
    count, packed, width = back_ref.shape
    rows = cache_ref.shape[3]
    request_rows = attention_ref.shape[0]
    parts = attention_ref.shape[1] // (count * width)
    kept = rows - (packed - parts * request_rows)
    ride = pltpu.make_async_copy(
        back_ref.at[:, parts * request_rows :], cache_ref.at[1, 0, :, kept:], sems.at[0]
    )
    ride.start()
    for s in range(count):
        block = back_ref[s, : parts * request_rows].astype(jnp.float32)
        for t in range(parts):
            attention_ref[:, (s * parts + t) * width : (s * parts + t + 1) * width] = block[
                t * request_rows : (t + 1) * request_rows
            ].astype(jnp.bfloat16)
    out = pltpu.make_async_copy(attention_ref, stored_attention, sems.at[1])
    out.start()
    ride.wait()
    out.wait()


def local(new_kv, old_keys, old_values, suffix_keys, suffix_values, queries, lengths, assign):
    seq_count = lax.axis_size("seq")
    core_count = lax.axis_size("pd")
    if seq_count > KVH or seq_count & (seq_count - 1):
        return general(new_kv, old_keys, old_values, suffix_keys, suffix_values, queries, lengths, assign)
    half = seq_count // 2
    request_rows = queries.shape[0]
    prefix_rows = new_kv.shape[1]
    group_width = queries.shape[1] // seq_count
    width = new_kv.shape[2] // seq_count
    prefix_length = prefix_rows * seq_count * core_count // NPFX
    rates = pl.pallas_call(
        rates_kernel,
        out_shape=pltpu.VMEM((8, HD), jnp.float32),
        out_specs=VMEM,
        cost_estimate=pl.CostEstimate(flops=2**33, bytes_accessed=1000, transcendentals=0),
    )()
    queries, rates = lax.optimization_barrier((queries, rates))

    def swap(x, k):
        return lax.ppermute(x, "seq", [(i, i ^ k) for i in range(seq_count)])

    asked = lax.all_to_all(
        queries.reshape(request_rows, seq_count, group_width).transpose(1, 0, 2), "seq", 0, 0, tiled=True
    )
    early = (old_keys, suffix_keys, old_values)
    late = (suffix_values,)
    riding = 32
    piece = (2, 2 * prefix_rows - riding, width)
    packed = NQH // KVH * request_rows + riding
    *kv_cuts, ride = pl.pallas_call(
        functools.partial(prepare_kernel, seq_count, core_count, prefix_length, riding),
        out_shape=[pltpu.VMEM(piece, jnp.bfloat16)] * half + [pltpu.VMEM((seq_count, riding, width), jnp.bfloat16)],
        in_specs=[VMEM] * 2,
        out_specs=[VMEM] * (half + 1),
        cost_estimate=pl.CostEstimate(flops=2**33, bytes_accessed=1000, transcendentals=0),
        compiler_params=pltpu.CompilerParams(vmem_limit_bytes=16 * 2**20),
    )(pin(rates), pin(new_kv))
    kv_near = [kv_cuts[0]]
    for j in range(1, half):
        kv_near.append(swap(kv_cuts[j], 2 * j))
    attended = pl.pallas_call(
        functools.partial(attend_kernel, core_count),
        out_shape=pltpu.HBM((seq_count, packed, width), jnp.bfloat16),
        in_specs=[VMEM] + [HBM] * (2 + len(late)) + [VMEM] * (len(early) + 1),
        out_specs=HBM,
        scratch_shapes=[
            *(pltpu.VMEM(x.shape, x.dtype) for x in late),
            pltpu.VMEM((seq_count, packed - riding, width), jnp.bfloat16),
            pltpu.VMEM((1, assign.shape[0]), jnp.int32),
            pltpu.VMEM((1, assign.shape[0]), jnp.int32),
            pltpu.SemaphoreType.DMA((len(late), 4)),
            pltpu.SemaphoreType.DMA((4,)),
        ],
        compiler_params=pltpu.CompilerParams(vmem_limit_bytes=16 * 2**20),
        cost_estimate=pl.CostEstimate(flops=2**30, bytes_accessed=2**20, transcendentals=2**10),
    )(
        pin(asked),
        *(pin(x, pltpu.HBM) for x in (assign.reshape(1, -1), lengths.reshape(1, -1), *late)),
        *(pin(x) for x in early),
        pin(ride),
    )
    kv_far = swap(forward(kv_near), 1)
    back = lax.all_to_all(attended, "seq", 0, 0, tiled=True)
    cache_shape = (2, 1, seq_count, prefix_rows, width)
    cache = pl.pallas_call(
        functools.partial(near_kernel, seq_count),
        out_shape=pltpu.HBM(cache_shape, jnp.bfloat16),
        in_specs=[VMEM] * half,
        out_specs=HBM,
        scratch_shapes=[pltpu.SemaphoreType.DMA((half, 2))],
        cost_estimate=pl.CostEstimate(flops=2**30, bytes_accessed=2**20, transcendentals=0),
    )(*(pin(x) for x in kv_near))
    cache = pl.pallas_call(
        functools.partial(far_kernel, seq_count),
        out_shape=pltpu.HBM(cache_shape, jnp.bfloat16),
        in_specs=[VMEM, HBM],
        out_specs=HBM,
        scratch_shapes=[pltpu.SemaphoreType.DMA((half, 2))],
        input_output_aliases={1: 0},
        cost_estimate=pl.CostEstimate(flops=2**30, bytes_accessed=2**20, transcendentals=0),
    )(pin(kv_far), cache)
    return tuple(
        pl.pallas_call(
            finish_kernel,
            out_shape=(
                pltpu.HBM(cache_shape, jnp.bfloat16),
                pltpu.HBM((request_rows, NQH * HD), jnp.bfloat16),
            ),
            in_specs=[VMEM, HBM],
            out_specs=(HBM, HBM),
            scratch_shapes=[
                pltpu.VMEM((request_rows, NQH * HD), jnp.bfloat16),
                pltpu.SemaphoreType.DMA((2,)),
            ],
            input_output_aliases={1: 0},
            cost_estimate=pl.CostEstimate(flops=0, bytes_accessed=2**20, transcendentals=0),
        )(pin(back), cache)
    )


def solution(mesh):
    return jax.shard_map(
        local,
        mesh=mesh,
        in_specs=(
            P("grp", ("seq", "pd"), None),
            P("seq", "grp", None),
            P("seq", "grp", None),
            P("pd", "seq", "grp", None, None),
            P("pd", "seq", "grp", None, None),
            P(("seq", "pd"), "grp"),
            P("grp"),
            P("grp"),
        ),
        out_specs=(P(None, "seq", "grp", "pd", None), P(("seq", "pd"), "grp")),
        check_vma=False,
    )
```
